32 devices in a mesh: groups: 2 (over y), adapter: 4 (over z), tensor: 2 (over x), seq: 2 (over core).
Axes of the slice: x: 2, y: 2, z: 4, core: 2. Of those that a mesh axis runs over, the one named last changes fastest.
Arguments:
- hidden: bfloat16 [256, 28672], P(('groups', 'adapter'), ('tensor', 'seq')), parts along dimension 0, may hold values from -6 to 6
- down_matrix: bfloat16 [28672, 8192], P(('tensor', 'seq'), 'adapter'), may hold values from -0.03125 to 0.03125
- adapter_first_factors: bfloat16 [8, 28672, 64], P('adapter', ('tensor', 'seq')), may hold values from -0.03125 to 0.03125
- adapter_second_factors: bfloat16 [8, 64, 8192], P('adapter'), may hold values from -0.75 to 0.75
- adapter_index_rows: int32 [256], P('groups'), parts along dimension 0, may hold values from 0 to 7, as said below
- storage: int32 [16], P('groups'), parts along dimension 0, may hold values from 0 to 7, as said below
Outputs:
- projected: bfloat16 [256, 8192], P(('groups', 'tensor', 'seq'), 'adapter'), parts along dimension 0
The draws below stay inside these ranges and needn't reach their ends.
There are 2 independent parts, one for each index of `groups`. The reference program is written for one: setup_inputs(seed, part) draws one part's arguments, and reference() takes and returns one part's arrays. A program takes and returns all parts, laid end to end along the dimension named above; an argument that names none is the same for every part. Nothing has to cross between parts.
Inputs may be any that keep to these rules, and one draw needn't show every extreme that they name: A permutation of the storage positions; position p lives on index p // 2 of adapter. `adapter_index_rows`: in each aligned block of 32 rows at most 16 rows name adapters stored on one index of adapter; in every draw one index receives exactly 16 rows from every block.
All inputs are finite; a program needn't handle non-finite values.
Results may differ from the reference program's by a relative error of at most 0.0049.
Values may be sent and summed in bfloat16 or wider, within the bound.
No kernel may reach another device: no remote copies, remote signals or barrier semaphores. Data moves between devices by JAX's collectives and lax.ppermute only.
A program may use at most 128 MiB of HBM per device.

```python
import jax
import jax.numpy as jnp
from jax import lax

MODEL_WIDTH = 8192
HIDDEN_UNITS = 28672
ADAPTER_RANK = 64
ADP_DEV = 2
RA = 32
CAP = 16
ROWS = 128
ADAPTER_COUNT = 8
N_ADAPTER = 4


def shared_positions(key):
    return jax.random.permutation(jax.random.fold_in(key, 11), ADAPTER_COUNT).astype(jnp.int32)


def draw_storage(key, part):
    return shared_positions(key)


def draw_adapter_index_rows(key, part):
    positions = shared_positions(key)
    key = jax.random.fold_in(key, 3)
    stored_at = jnp.zeros((ADAPTER_COUNT,), jnp.int32).at[positions].set(jnp.arange(ADAPTER_COUNT, dtype=jnp.int32))
    hot_owner = jax.random.randint(jax.random.fold_in(key, 1), (), 0, N_ADAPTER).astype(jnp.int32)
    owner_pool = jnp.repeat(jnp.arange(N_ADAPTER, dtype=jnp.int32), CAP - 1)
    pool_size = owner_pool.shape[0]

    def one_block(block_key):
        key_order, key_shuffle, key_local = jax.random.split(block_key, 3)
        scores = jax.random.permutation(key_order, pool_size).astype(jnp.int32)
        scores = jnp.where(owner_pool == hot_owner, scores + pool_size, scores)
        ordering = jnp.argsort(scores)
        chosen = owner_pool[ordering[:RA - CAP]]
        owner_rows = jnp.concatenate([jnp.full((CAP,), hot_owner, jnp.int32), chosen])
        owner_rows = jax.random.permutation(key_shuffle, owner_rows)
        local_index = jax.random.randint(key_local, (RA,), 0, ADP_DEV).astype(jnp.int32)
        return stored_at[owner_rows * ADP_DEV + local_index]
    block_keys = jax.random.split(jax.random.fold_in(key, 2), N_ADAPTER)
    return jax.vmap(one_block)(block_keys).reshape(-1).astype(jnp.int32)


def shard_levels(own_key, dims, pieces, least, top_value):
    loudness, own = 1.0, jax.random.fold_in(own_key, 6)
    for dim, blocks in pieces:
        steps = jnp.exp(jax.random.uniform(jax.random.fold_in(own, dim), (blocks,), jnp.float32, least / len(pieces), top_value / len(pieces)))
        loudness = loudness * jnp.repeat(steps, dims[dim] // blocks).reshape([-1 if axis == dim else 1 for axis in range(len(dims))])
    return loudness


def gaussian(rng, extent, deviation, most, pieces=(), held_as=jnp.bfloat16):
    loudness = shard_levels(rng, extent, pieces, -0.22, 0.18) if pieces else 1.0
    drawn = jax.random.normal(rng, extent, jnp.float32) * deviation * loudness
    return jnp.minimum(jnp.maximum(drawn, -most), most).astype(held_as)


def setup_inputs(seed: int = 0, part: int = 0) -> dict:
    splits = jax.random.split(jax.random.key(seed), 7)
    own_keys = jax.random.split(jax.random.fold_in(splits[6], part), 7)
    return {
        "hidden": gaussian(own_keys[0], (ROWS, HIDDEN_UNITS), 1.0, 6.0, ((0, 4), (1, 4))),
        "down_matrix": gaussian(splits[1], (HIDDEN_UNITS, MODEL_WIDTH), HIDDEN_UNITS ** -0.5, 0.03125, ((0, 4), (1, 4))),
        "adapter_first_factors": gaussian(splits[2], (ADAPTER_COUNT, HIDDEN_UNITS, ADAPTER_RANK), HIDDEN_UNITS ** -0.5, 0.03125, ((0, 4), (1, 4))),
        "adapter_second_factors": gaussian(splits[3], (ADAPTER_COUNT, ADAPTER_RANK, MODEL_WIDTH), ADAPTER_RANK ** -0.5, 0.75, ((0, 4),)),
        "adapter_index_rows": draw_adapter_index_rows(jax.random.fold_in(jax.random.fold_in(splits[6], part), 71), part),
        "storage": draw_storage(jax.random.fold_in(jax.random.fold_in(splits[6], part), 71), part),
    }


def reference(hidden, down_matrix, adapter_first_factors, adapter_second_factors, adapter_index_rows, storage):
    base_out = jnp.dot(hidden, down_matrix, preferred_element_type=jnp.float32)
    position = storage[adapter_index_rows].astype(jnp.int32)
    row_blocks = hidden.reshape(N_ADAPTER, RA, HIDDEN_UNITS)
    position_blocks = position.reshape(N_ADAPTER, RA)

    def block_delta(item):
        rows_here, present_position_mask = item
        first_lowrank_matrix = adapter_first_factors[present_position_mask].astype(jnp.float32)
        low_rank = jnp.einsum("rf,rfk->rk", rows_here.astype(jnp.float32), first_lowrank_matrix)
        low_rank = low_rank.astype(jnp.bfloat16)
        second_lowrank_matrix = adapter_second_factors[present_position_mask].astype(jnp.float32)
        delta_rows = jnp.einsum("rk,rkd->rd", low_rank.astype(jnp.float32), second_lowrank_matrix)
        return delta_rows.astype(jnp.bfloat16)

    delta_rows = lax.map(block_delta, (row_blocks, position_blocks)).reshape(ROWS, MODEL_WIDTH)
    delta_rows = lax.optimization_barrier(delta_rows)
    return (base_out + delta_rows.astype(jnp.float32)).astype(jnp.bfloat16)
```

```python
import functools

import jax
import jax.numpy as jnp
from jax import lax
from jax.experimental import pallas as pl
from jax.experimental.pallas import tpu as pltpu
from jax.sharding import PartitionSpec as P

F32 = jnp.float32
BF16 = jnp.bfloat16
VMEM_LIMIT = 40 * 1024 * 1024


def tile_of(extent, most):
    tile = most
    while extent % tile:
        tile //= 2
    return tile


def gathered(refs):
    return jnp.concatenate([ref[...] for ref in refs], axis=0)


def dot_nt(a, b):
    return lax.dot_general(a, b, (((1,), (1,)), ((), ())), preferred_element_type=F32)


def first_kernel(h0, h1, h2, h3, w_ref, a_ref, base_ref, low_ref):
    @pl.when(pl.program_id(0) == 0)
    def _():
        base_ref[...] = jnp.zeros_like(base_ref)
        low_ref[...] = jnp.zeros_like(low_ref)

    h = gathered((h0, h1, h2, h3))
    base_ref[...] += jnp.dot(h, w_ref[...], preferred_element_type=F32)
    low_ref[...] += dot_nt(h, a_ref[...])


def first_half(blocks, w, a, offset):
    rows, extent = blocks[0].shape
    width = w.shape[1]
    low = a.shape[0]
    tile = tile_of(extent, 512)
    skip = offset // tile
    count = len(blocks)
    return pl.pallas_call(
        first_kernel,
        grid=(extent // tile,),
        in_specs=[pl.BlockSpec((rows, tile), lambda k: (0, k))] * count
        + [
            pl.BlockSpec((tile, width), lambda k: (k + skip, 0)),
            pl.BlockSpec((low, tile), lambda k: (0, k + skip)),
        ],
        out_specs=[
            pl.BlockSpec((count * rows, width), lambda k: (0, 0)),
            pl.BlockSpec((count * rows, low), lambda k: (0, 0)),
        ],
        out_shape=[
            jax.ShapeDtypeStruct((count * rows, width), F32),
            jax.ShapeDtypeStruct((count * rows, low), F32),
        ],
        compiler_params=pltpu.CompilerParams(vmem_limit_bytes=VMEM_LIMIT),
        cost_estimate=pl.CostEstimate(
            flops=2 * count * rows * extent * (width + low),
            bytes_accessed=2 * extent * (width + low + count * rows) + 4 * count * rows * width,
            transcendentals=0,
        ),
        name="first_half",
    )(*blocks, w, a)


def low_kernel(pick, h0, h1, h2, h3, a_ref, low_in, keep_ref, send_ref, total):
    step = pl.program_id(0)

    @pl.when(step == 0)
    def _():
        total[...] = low_in[...]

    part = dot_nt(gathered((h0, h1, h2, h3)), a_ref[...])
    total[...] += part.reshape(total.shape)

    @pl.when(step == pl.num_programs(0) - 1)
    def _():
        mine = pick[0]
        for far in range(2):
            keep_ref[far] = total[2 * far + mine]
            send_ref[far] = total[2 * far + 1 - mine]


def second_low(pick, blocks, a, low_in, offset):
    rows, extent = blocks[0].shape
    low = a.shape[0]
    tile = tile_of(extent, 2048)
    skip = offset // tile
    return pl.pallas_call(
        low_kernel,
        grid_spec=pltpu.PrefetchScalarGridSpec(
            num_scalar_prefetch=1,
            grid=(extent // tile,),
            in_specs=[pl.BlockSpec((rows, tile), lambda k, s: (0, k))] * 4
            + [
                pl.BlockSpec((low, tile), lambda k, s: (0, k + skip)),
                pl.BlockSpec((4, rows, low), lambda k, s: (0, 0, 0)),
            ],
            out_specs=[pl.BlockSpec((2, rows, low), lambda k, s: (0, 0, 0))] * 2,
            scratch_shapes=[pltpu.VMEM((4, rows, low), F32)],
        ),
        out_shape=[jax.ShapeDtypeStruct((2, rows, low), F32)] * 2,
        compiler_params=pltpu.CompilerParams(vmem_limit_bytes=VMEM_LIMIT),
        cost_estimate=pl.CostEstimate(
            flops=8 * rows * extent * low,
            bytes_accessed=2 * extent * (low + 4 * rows),
            transcendentals=0,
        ),
        name="second_low",
    )(pick, *blocks, a, low_in.reshape(4, rows, low))


def base_kernel(pick, h0, h1, h2, h3, w_ref, base_in, keep_ref, send_ref, total):
    step = pl.program_id(0)

    @pl.when(step == 0)
    def _():
        total[...] = base_in[...]

    part = jnp.dot(gathered((h0, h1, h2, h3)), w_ref[...], preferred_element_type=F32)
    total[...] += part.reshape(total.shape)

    @pl.when(step == pl.num_programs(0) - 1)
    def _():
        mine = pick[0]
        for far in range(2):
            keep_ref[far] = total[2 * far + mine]
            send_ref[far] = total[2 * far + 1 - mine].astype(BF16)


def second_base(pick, blocks, w, base_in, offset):
    rows, extent = blocks[0].shape
    width = w.shape[1]
    tile = tile_of(extent, 512)
    skip = offset // tile
    return pl.pallas_call(
        base_kernel,
        grid_spec=pltpu.PrefetchScalarGridSpec(
            num_scalar_prefetch=1,
            grid=(extent // tile,),
            in_specs=[pl.BlockSpec((rows, tile), lambda k, s: (0, k))] * 4
            + [
                pl.BlockSpec((tile, width), lambda k, s: (k + skip, 0)),
                pl.BlockSpec((4, rows, width), lambda k, s: (0, 0, 0)),
            ],
            out_specs=[pl.BlockSpec((2, rows, width), lambda k, s: (0, 0, 0))] * 2,
            scratch_shapes=[pltpu.VMEM((4, rows, width), F32)],
        ),
        out_shape=[
            jax.ShapeDtypeStruct((2, rows, width), F32),
            jax.ShapeDtypeStruct((2, rows, width), BF16),
        ],
        compiler_params=pltpu.CompilerParams(vmem_limit_bytes=VMEM_LIMIT),
        cost_estimate=pl.CostEstimate(
            flops=8 * rows * extent * width,
            bytes_accessed=2 * extent * (width + 4 * rows) + 8 * rows * width,
            transcendentals=0,
        ),
        name="second_base",
    )(pick, *blocks, w, base_in.reshape(4, rows, width))


def swap_kernel(pick, keep_in, came, keep_ref, send_ref):
    mine = pick[0]
    keep_ref[...] = keep_in[mine] + came[mine].astype(F32)
    send_ref[...] = (keep_in[1 - mine] + came[1 - mine].astype(F32)).astype(send_ref.dtype)


def split_sum(pick, keep, came):
    shape = keep.shape[1:]
    return pl.pallas_call(
        swap_kernel,
        in_specs=[
            pl.BlockSpec(memory_space=pltpu.SMEM),
            pl.BlockSpec(memory_space=pltpu.VMEM),
            pl.BlockSpec(memory_space=pltpu.VMEM),
        ],
        out_specs=[pl.BlockSpec(memory_space=pltpu.VMEM)] * 2,
        out_shape=[jax.ShapeDtypeStruct(shape, F32), jax.ShapeDtypeStruct(shape, came.dtype)],
        name="split_sum",
    )(pick, keep, came)


def widen_kernel(own, low_a, low_b, owner_row, local_row, rank_row, b_ref, out_ref, *, slots, stored):
    low = (low_a[...] + low_b[...]).astype(BF16)
    rows = low.shape[0]
    slot = lax.broadcasted_iota(jnp.int32, (slots, rows), 0)
    here = (owner_row[...] == own[0]) & (rank_row[...] == slot)
    rank_extent = low.shape[1] // stored
    terms = []
    for index in range(stored):
        taken = jnp.where(here & (local_row[...] == index), 1.0, 0.0).astype(BF16)
        terms.append(
            jnp.dot(
                taken,
                low[:, index * rank_extent : (index + 1) * rank_extent],
                preferred_element_type=F32,
            ).astype(BF16)
        )
    packed = jnp.concatenate(terms, axis=1)
    owners, _, width = out_ref.shape
    for part in range(owners):
        out_ref[part] = jnp.dot(
            packed, b_ref[:, part * width : (part + 1) * width], preferred_element_type=F32
        ).astype(BF16)


def widen(own, low_a, low_b, owner_row, local_row, rank_row, b, slots, stored, owners):
    width = b.shape[1] // owners
    return pl.pallas_call(
        functools.partial(widen_kernel, slots=slots, stored=stored),
        in_specs=[pl.BlockSpec(memory_space=pltpu.SMEM)]
        + [pl.BlockSpec(memory_space=pltpu.VMEM)] * 6,
        out_specs=pl.BlockSpec(memory_space=pltpu.VMEM),
        out_shape=jax.ShapeDtypeStruct((owners, slots, width), BF16),
        compiler_params=pltpu.CompilerParams(vmem_limit_bytes=VMEM_LIMIT),
        name="widen",
    )(own, low_a, low_b, owner_row, local_row, rank_row, b)


def last_kernel(own, keep, came, owner_col, rank_col, d0, d1, d2, d3, out_ref):
    slots = d0.shape[0]
    rows = keep.shape[0]
    slot = lax.broadcasted_iota(jnp.int32, (rows, slots), 1)
    total = keep[...] + came[...].astype(F32)
    picks = []
    for step in range(4):
        owner = lax.rem(own[0] + 4 - step, 4)
        picks.append(
            jnp.where((owner_col[...] == owner) & (rank_col[...] == slot), 1.0, 0.0).astype(BF16)
        )
    picked = jnp.concatenate(picks, axis=1)
    rows_back = gathered((d0, d1, d2, d3))
    delta = jnp.dot(picked, rows_back, preferred_element_type=F32)
    out_ref[...] = (total + delta).astype(out_ref.dtype)


def last(own, keep, came, owner_col, rank_col, deltas):
    return pl.pallas_call(
        last_kernel,
        in_specs=[pl.BlockSpec(memory_space=pltpu.SMEM)]
        + [pl.BlockSpec(memory_space=pltpu.VMEM)] * 8,
        out_specs=pl.BlockSpec(memory_space=pltpu.VMEM),
        out_shape=jax.ShapeDtypeStruct(keep.shape, BF16),
        name="last",
    )(own, keep, came, owner_col, rank_col, *deltas)


def small_body(
    hidden, down_matrix, adapter_first_factors, adapter_second_factors, adapter_index_rows, storage
):
    owners = 4
    rows, extent = hidden.shape
    stored, _, rank_extent = adapter_first_factors.shape
    adapters = storage.shape[0]
    slots = max(2, min(rows // 2, 2 * rows // owners))
    own = lax.axis_index("adapter")
    far = lax.axis_index("tensor")
    near = lax.axis_index("seq")
    part = far * 2 + near
    half = extent // 2

    a = jnp.swapaxes(adapter_first_factors, 1, 2).reshape(stored * rank_extent, extent)
    b = adapter_second_factors.reshape(stored * rank_extent, -1)
    near_pick = jnp.reshape(near ^ (own & 1), (1,)).astype(jnp.int32)
    far_pick = jnp.reshape(far ^ (own >> 1), (1,)).astype(jnp.int32)
    own_ref = jnp.reshape(own, (1,)).astype(jnp.int32)

    pairs = [(0, 1), (1, 0), (2, 3), (3, 2)]
    twos = [(0, 2), (2, 0), (1, 3), (3, 1)]
    both = [(0, 1), (1, 0)]
    hop = functools.partial(lax.ppermute, axis_name="adapter")

    parts = [hidden[:, :half], hidden[:, half:]]
    h2a = hop(parts[0], perm=twos)
    h1a = hop(parts[0], perm=pairs)
    h2b = hop(parts[1], perm=twos)
    h1b = hop(parts[1], perm=pairs)
    h3a = hop(h2a, perm=pairs)
    h3b = hop(h2b, perm=pairs)
    blocks_a = (parts[0], h1a, h2a, h3a)
    blocks_b = (parts[1], h1b, h2b, h3b)

    mine = lax.dynamic_slice_in_dim(adapter_index_rows, part * rows, rows, 0)
    match = mine[:, None] == jnp.arange(adapters, dtype=jnp.int32)[None, :]
    position = jnp.sum(jnp.where(match, storage[None, :], 0), axis=1)
    owner = position // stored
    local = position % stored
    index = jnp.arange(rows, dtype=jnp.int32)
    rank = jnp.sum(
        ((owner[:, None] == owner[None, :]) & (index[None, :] < index[:, None])).astype(jnp.int32),
        axis=1,
    )

    base_a, low_a = first_half(blocks_a, down_matrix, a, 0)
    low_keep, low_send = second_low(near_pick, blocks_b, a, low_a, half)
    low_came = lax.ppermute(low_send, "seq", both)
    low_keep, low_send = split_sum(far_pick, low_keep, low_came)
    low_came = lax.ppermute(low_send, "tensor", both)

    base_keep, base_send = second_base(near_pick, blocks_b, down_matrix, base_a, half)
    base_came = lax.ppermute(base_send, "seq", both)
    base_keep, base_send = split_sum(far_pick, base_keep, base_came)
    base_came = lax.ppermute(base_send, "tensor", both)

    wide = widen(
        own_ref, low_keep, low_came, owner[None, :], local[None, :], rank[None, :], b,
        slots, stored, owners,
    )
    deltas = [lax.dynamic_index_in_dim(wide, own, 0, keepdims=False)]
    for step in range(1, owners):
        block = lax.dynamic_index_in_dim(wide, (own + step) % owners, 0, keepdims=False)
        deltas.append(hop(block, perm=[(i, (i + step) % owners) for i in range(owners)]))
    return last(own_ref, base_keep, base_came, owner[:, None], rank[:, None], deltas)


def body(
    hidden, down_matrix, adapter_first_factors, adapter_second_factors, adapter_index_rows, storage
):
    owners = lax.axis_size("adapter")
    groups = lax.axis_size(("tensor", "seq"))
    block_of_rows = hidden.shape[0]
    slice_width = hidden.shape[1]
    stored_factors = adapter_first_factors.shape[0]
    rank_extent = adapter_first_factors.shape[2]
    adapters = storage.shape[0]
    capacity = max(2, min(block_of_rows // 2, 2 * block_of_rows // owners))
    present_block_list = owners // groups
    own_index = lax.axis_index("adapter")
    part_index = lax.axis_index(("tensor", "seq"))
    id_match = adapter_index_rows[:, None] == jnp.arange(adapters, dtype=jnp.int32)[None, :]
    position = jnp.sum(jnp.where(id_match, storage[None, :], 0), axis=1)
    owner_blocks = (position // stored_factors).reshape(owners, block_of_rows)
    local_blocks = (position % stored_factors).reshape(owners, block_of_rows)
    owner_hits = (
        owner_blocks[:, :, None] == jnp.arange(owners, dtype=jnp.int32)[None, None, :]
    ).astype(jnp.int32)
    slot_rank = jnp.sum(owner_hits * (jnp.cumsum(owner_hits, axis=1) - 1), axis=2)
    slot_of = owner_blocks * capacity + slot_rank
    slot_range = jnp.arange(capacity, dtype=jnp.int32)
    owned = owner_blocks == own_index
    picker = owned[:, None, :] & (slot_rank[:, None, :] == slot_range[None, :, None])
    local_in = jnp.sum(jnp.where(picker, local_blocks[:, None, :], 0), axis=2)
    h_all = lax.all_gather(hidden, "adapter", axis=0, tiled=True)
    partial_total = lax.psum_scatter(
        jnp.dot(h_all, down_matrix, preferred_element_type=jnp.float32),
        ("tensor", "seq"),
        scatter_dimension=0,
        tiled=True,
    )
    my_slots = lax.dynamic_index_in_dim(slot_of, own_index, 0, keepdims=False)
    send_pick = my_slots[None, :] == jnp.arange(owners * capacity, dtype=jnp.int32)[:, None]
    send_rows = jnp.dot(send_pick.astype(jnp.bfloat16), hidden, preferred_element_type=jnp.float32)
    send_rows = send_rows.astype(jnp.bfloat16).reshape(owners, capacity, slice_width)
    input_rows = lax.all_to_all(send_rows, "adapter", split_axis=0, concat_axis=0, tiled=True)
    product_terms = jnp.einsum(
        "mbw,twk->mbtk", input_rows, adapter_first_factors, preferred_element_type=jnp.float32
    )
    product_terms = product_terms.reshape(
        input_rows.shape[0], input_rows.shape[1], stored_factors * rank_extent
    )
    select_low = (
        local_in[:, :, None] == jnp.arange(stored_factors, dtype=jnp.int32)[None, None, :]
    ).astype(jnp.float32)
    low_part = jnp.sum(
        product_terms.reshape(owners, capacity, stored_factors, rank_extent)
        * select_low[:, :, :, None],
        axis=2,
    )
    low_rank = lax.psum(low_part, ("tensor", "seq")).astype(jnp.bfloat16)
    owned_lowrank_part = lax.dynamic_slice_in_dim(
        low_rank, part_index * present_block_list, present_block_list, 0
    )
    mine_local = lax.dynamic_slice_in_dim(
        local_in, part_index * present_block_list, present_block_list, 0
    )
    widened_rows = jnp.einsum(
        "jwf,sfe->jwse",
        owned_lowrank_part,
        adapter_second_factors,
        preferred_element_type=jnp.float32,
    )
    select_out = (
        mine_local[:, :, None] == jnp.arange(stored_factors, dtype=jnp.int32)[None, None, :]
    ).astype(jnp.float32)
    delta_rows = jnp.sum(widened_rows * select_out[:, :, :, None], axis=2).astype(jnp.bfloat16)
    returned_rows = lax.all_to_all(delta_rows, "adapter", split_axis=2, concat_axis=1, tiled=True)
    my_targets = lax.dynamic_slice_in_dim(
        slot_of, part_index * present_block_list, present_block_list, 0
    )
    target_pick = (
        my_targets[:, :, None] == jnp.arange(owners * capacity, dtype=jnp.int32)[None, None, :]
    ).astype(jnp.bfloat16)
    adapter_delta_rows = jnp.einsum(
        "prs,psd->prd", target_pick, returned_rows, preferred_element_type=jnp.float32
    )
    adapter_delta_rows = adapter_delta_rows.reshape(
        present_block_list * block_of_rows, returned_rows.shape[2]
    )
    return (partial_total + adapter_delta_rows).astype(jnp.bfloat16)


def solution(mesh):
    placed = (
        P(("groups", "adapter"), ("tensor", "seq")),
        P(("tensor", "seq"), "adapter"),
        P("adapter", ("tensor", "seq"), None),
        P("adapter", None, None),
        P("groups"),
        P("groups"),
    )
    small = mesh.shape["adapter"] == 4 and mesh.shape["tensor"] == 2 and mesh.shape["seq"] == 2
    return jax.shard_map(
        small_body if small else body,
        mesh=mesh,
        in_specs=placed,
        out_specs=P(("groups", "tensor", "seq"), "adapter"),
        check_vma=False,
    )
```

```python
import functools

import jax
import jax.numpy as jnp
from jax import lax
from jax.experimental import pallas as pl
from jax.experimental.pallas import tpu as pltpu
from jax.sharding import PartitionSpec as P

F32 = jnp.float32
BF16 = jnp.bfloat16
MIB = 1024 * 1024
VMEM = pl.BlockSpec(memory_space=pltpu.VMEM)
SMEM = pl.BlockSpec(memory_space=pltpu.SMEM)
HBM = pl.BlockSpec(memory_space=pltpu.HBM)
COLUMNS = 512
FETCH_MIB = 27
SHARE = 8


def params(limit):
    return pltpu.CompilerParams(vmem_limit_bytes=limit * MIB)


def cost(flops, moved):
    return pl.CostEstimate(flops=int(flops), bytes_accessed=int(moved), transcendentals=0)


def fetch_kernel(*refs, pieces):
    count = len(pieces)
    sources, targets, sems = refs[:count], refs[count : 2 * count], refs[2 * count]
    copies = []
    for source, target, (axis, start, length, cuts) in zip(sources, targets, pieces):
        step = length // cuts
        for cut in range(cuts):
            if axis == 0:
                from_ref = source.at[pl.ds(start + cut * step, step)]
                to_ref = target.at[pl.ds(cut * step, step)]
            else:
                from_ref = source.at[:, pl.ds(start + cut * step, step)]
                to_ref = target.at[:, pl.ds(cut * step, step)]
            copies.append(pltpu.make_async_copy(from_ref, to_ref, sems.at[len(copies)]))
    for copy in copies:
        copy.start()
    for copy in copies:
        copy.wait()


def fetch(arrays, pieces, name):
    shapes = []
    for array, (axis, _, length, _) in zip(arrays, pieces):
        shape = list(array.shape)
        shape[axis] = length
        shapes.append(pltpu.VMEM(tuple(shape), array.dtype))
    moved = sum(2 * s.shape[0] * s.shape[1] for s in shapes)
    total = sum(piece[3] for piece in pieces)
    return pl.pallas_call(
        functools.partial(fetch_kernel, pieces=pieces),
        in_specs=[HBM] * len(arrays),
        out_specs=[VMEM] * len(arrays),
        out_shape=shapes,
        scratch_shapes=[pltpu.SemaphoreType.DMA((total,))],
        compiler_params=params(FETCH_MIB),
        cost_estimate=cost(0, moved),
        name=name,
    )(*arrays)


def dot_nt(a, b):
    return lax.dot_general(a, b, (((1,), (1,)), ((), ())), preferred_element_type=F32)


def ordered(picks, blocks):
    near, far = picks[0] == 1, picks[1] == 1
    b0, b1, b2, b3 = [block[...] for block in blocks]
    k0, k2 = jnp.where(near, b1, b0), jnp.where(near, b3, b2)
    s0, s2 = jnp.where(near, b0, b1), jnp.where(near, b2, b3)
    return jnp.concatenate(
        [
            jnp.where(far, k2, k0),
            jnp.where(far, k0, k2),
            jnp.where(far, s2, s0),
            jnp.where(far, s0, s2),
        ],
        axis=0,
    )


def first_kernel(
    picks, b0, b1, b2, b3, w_far, w_ref, a_ref, base_ref, low_ref, streamed, sems, *, cuts
):
    cut = streamed.shape[0]
    step = cut // cuts
    copies = []
    for index in range(cuts):
        rows = pl.ds(index * step, step)
        copies.append(pltpu.make_async_copy(w_far.at[rows], streamed.at[rows], sems.at[index]))
        copies[-1].start()
    h = ordered(picks, (b0, b1, b2, b3))
    depth = h.shape[1]
    low_ref[...] = dot_nt(h, a_ref[:, :depth])
    for start in range(0, w_ref.shape[1], COLUMNS):
        columns = slice(start, start + COLUMNS)
        base_ref[:, columns] = jnp.dot(h[:, cut:], w_ref[:, columns], preferred_element_type=F32)
    for copy in copies:
        copy.wait()
    for start in range(0, w_ref.shape[1], COLUMNS):
        columns = slice(start, start + COLUMNS)
        base_ref[:, columns] += jnp.dot(
            h[:, :cut], streamed[:, columns], preferred_element_type=F32
        )


def first_half(picks, blocks, w_far, w, a, cut):
    rows, extent = blocks[0].shape
    width, low = w.shape[1], a.shape[0]
    cuts = 4
    return pl.pallas_call(
        functools.partial(first_kernel, cuts=cuts),
        in_specs=[SMEM] + [VMEM] * 4 + [HBM] + [VMEM] * 2,
        out_specs=[VMEM] * 2,
        out_shape=[
            jax.ShapeDtypeStruct((4 * rows, width), F32),
            jax.ShapeDtypeStruct((4 * rows, low), F32),
        ],
        scratch_shapes=[pltpu.VMEM((cut, width), BF16), pltpu.SemaphoreType.DMA((cuts,))],
        compiler_params=params(20),
        cost_estimate=cost(8 * rows * extent * (width + low), 4 * MIB),
        name="first_half",
    )(picks, *blocks, w_far, w, a)


def low_kernel(picks, b0, b1, b2, b3, a_ref, low_in, keep_ref, send_ref):
    h = ordered(picks, (b0, b1, b2, b3))
    skip = a_ref.shape[1] - h.shape[1]
    total = low_in[...] + dot_nt(h, a_ref[:, skip:])
    rows = keep_ref.shape[0]
    keep_ref[...] = total[:rows]
    send_ref[...] = total[rows:]


def second_low(picks, blocks, a, low_in):
    rows, extent = blocks[0].shape
    low = a.shape[0]
    return pl.pallas_call(
        low_kernel,
        in_specs=[SMEM] + [VMEM] * 6,
        out_specs=[VMEM] * 2,
        out_shape=[jax.ShapeDtypeStruct((2 * rows, low), F32)] * 2,
        compiler_params=params(8),
        cost_estimate=cost(8 * rows * extent * low, MIB),
        name="second_low",
    )(picks, *blocks, a, low_in)


def base_kernel(picks, b0, b1, b2, b3, w_ref, base_in, keep_ref, send_ref):
    h = ordered(picks, (b0, b1, b2, b3))
    rows = keep_ref.shape[0]
    skip = w_ref.shape[0] - h.shape[1]
    for start in range(0, w_ref.shape[1], COLUMNS):
        columns = slice(start, start + COLUMNS)
        part = jnp.dot(h, w_ref[skip:, columns], preferred_element_type=F32)
        total = base_in[:, columns] + part
        keep_ref[:, columns] = total[:rows]
        send_ref[:, columns] = total[rows:].astype(BF16)


def second_base(picks, blocks, w, base_in):
    rows, extent = blocks[0].shape
    width = w.shape[1]
    return pl.pallas_call(
        base_kernel,
        in_specs=[SMEM] + [VMEM] * 6,
        out_specs=[VMEM] * 2,
        out_shape=[
            jax.ShapeDtypeStruct((2 * rows, width), F32),
            jax.ShapeDtypeStruct((2 * rows, width), BF16),
        ],
        compiler_params=params(12),
        cost_estimate=cost(8 * rows * extent * width, 4 * MIB),
        name="second_base",
    )(picks, *blocks, w, base_in)


def split_kernel(keep_in, came, keep_ref, send_ref):
    rows = keep_ref.shape[0]
    total = keep_in[...] + came[...].astype(F32)
    keep_ref[...] = total[:rows]
    send_ref[...] = total[rows:].astype(send_ref.dtype)


def split_sum(keep, came, name):
    shape = (keep.shape[0] // 2, keep.shape[1])
    return pl.pallas_call(
        split_kernel,
        in_specs=[VMEM] * 2,
        out_specs=[VMEM] * 2,
        out_shape=[jax.ShapeDtypeStruct(shape, F32), jax.ShapeDtypeStruct(shape, came.dtype)],
        compiler_params=params(4),
        cost_estimate=cost(0, MIB),
        name=name,
    )(keep, came)


def plan_kernel(scalars, storage, row_ref, column_ref, into_ref, back_ref, *, stored, slots):
    own = scalars[0]
    rows = row_ref.shape[1]

    def position(index):
        found = jnp.zeros_like(index)
        for adapter in range(storage.shape[0]):
            found = jnp.where(index == adapter, storage[adapter], found)
        return found

    def owner_of(place):
        owner = jnp.zeros_like(place)
        for step in range(1, 4):
            owner += (place >= step * stored).astype(jnp.int32)
        return owner

    place_row, place_column = position(row_ref[...]), position(column_ref[...])
    owner_row, owner_column = owner_of(place_row), owner_of(place_column)
    local_row = place_row - owner_row * stored
    down = lax.broadcasted_iota(jnp.int32, (rows, rows), 0)
    across = lax.broadcasted_iota(jnp.int32, (rows, rows), 1)
    same = owner_column == owner_row
    rank_row = jnp.sum((same & (down < across)).astype(jnp.int32), axis=0, keepdims=True)
    rank_column = jnp.sum((same & (across < down)).astype(jnp.int32), axis=1, keepdims=True)
    slot = lax.broadcasted_iota(jnp.int32, (slots, rows), 0)
    here = (owner_row == own) & (rank_row == slot)
    for index in range(stored):
        taken = here & (local_row == index)
        into_ref[index] = jnp.where(taken, 1.0, 0.0).astype(BF16)
    lane = lax.broadcasted_iota(jnp.int32, (rows, 4 * slots), 1)
    hops = lax.rem(own + 4 - owner_column, 4)
    back_ref[...] = jnp.where(lane == hops * slots + rank_column, 1.0, 0.0).astype(BF16)


def plan(scalars, storage, mine, stored, slots):
    rows = mine.shape[0]
    return pl.pallas_call(
        functools.partial(plan_kernel, stored=stored, slots=slots),
        in_specs=[SMEM, SMEM, VMEM, VMEM],
        out_specs=[VMEM] * 2,
        out_shape=[
            jax.ShapeDtypeStruct((stored, slots, rows), BF16),
            jax.ShapeDtypeStruct((rows, 4 * slots), BF16),
        ],
        compiler_params=params(2),
        cost_estimate=cost(0, MIB),
        name="plan",
    )(scalars, storage, mine[None, :], mine[:, None])


def widen_kernel(scalars, low_a, low_b, into_ref, b_ref, *outs):
    low = (low_a[...] + low_b[...]).astype(BF16)
    stored = into_ref.shape[0]
    rank_extent = low.shape[1] // stored
    terms = []
    for index in range(stored):
        part = low[:, index * rank_extent : (index + 1) * rank_extent]
        terms.append(jnp.dot(into_ref[index], part, preferred_element_type=F32).astype(BF16))
    packed = jnp.concatenate(terms, axis=1)
    width = outs[0].shape[1]
    for step, out in enumerate(outs):
        start = pl.multiple_of(lax.rem(scalars[0] + step, len(outs)) * width, width)
        columns = b_ref[:, pl.ds(start, width)]
        out[...] = jnp.dot(packed, columns, preferred_element_type=F32).astype(BF16)


def widen(scalars, low_a, low_b, into, b, slots, owners):
    width = b.shape[1] // owners
    return pl.pallas_call(
        widen_kernel,
        in_specs=[SMEM] + [VMEM] * 4,
        out_specs=[VMEM] * owners,
        out_shape=[jax.ShapeDtypeStruct((slots, width), BF16)] * owners,
        compiler_params=params(6),
        cost_estimate=cost(0, MIB),
        name="widen",
    )(scalars, low_a, low_b, into, b)


def last_kernel(keep, came, back, d0, d1, d2, d3, out_ref):
    deltas = jnp.concatenate([d[...] for d in (d0, d1, d2, d3)], axis=0)
    delta = jnp.dot(back[...], deltas, preferred_element_type=F32)
    out_ref[...] = (keep[...] + came[...].astype(F32) + delta).astype(out_ref.dtype)


def last(keep, came, back, deltas):
    return pl.pallas_call(
        last_kernel,
        in_specs=[VMEM] * 7,
        out_specs=VMEM,
        out_shape=jax.ShapeDtypeStruct(keep.shape, BF16),
        compiler_params=params(4),
        cost_estimate=cost(0, MIB),
        name="last",
    )(keep, came, back, *deltas)


def small_body(
    hidden, down_matrix, adapter_first_factors, adapter_second_factors, adapter_index_rows, storage
):
    owners = 4
    rows, extent = hidden.shape
    stored, _, rank_extent = adapter_first_factors.shape
    slots = max(2, min(rows // 2, 2 * rows // owners))
    own = lax.axis_index("adapter")
    far = lax.axis_index("tensor")
    near = lax.axis_index("seq")
    part = far * 2 + near
    half = 256 * (extent * SHARE // (256 * 16))
    cut = half // 2
    rest = extent - half

    a = jnp.swapaxes(adapter_first_factors, 1, 2).reshape(stored * rank_extent, extent)
    b = adapter_second_factors.reshape(stored * rank_extent, -1)
    picks = jnp.stack([near ^ (own & 1), far ^ (own >> 1)]).astype(jnp.int32)
    scalars = jnp.reshape(own, (1,)).astype(jnp.int32)

    pairs = [(0, 1), (1, 0), (2, 3), (3, 2)]
    twos = [(0, 2), (2, 0), (1, 3), (3, 1)]
    both = [(0, 1), (1, 0)]
    hop = functools.partial(lax.ppermute, axis_name="adapter")

    mine = lax.dynamic_slice_in_dim(adapter_index_rows, part * rows, rows, 0)
    h0a, h0b = hidden[:, :half], hidden[:, half:]
    h2a = hop(h0a, perm=twos)
    h1a = hop(h0a, perm=pairs)
    into, back = plan(scalars, storage, mine, stored, slots)
    picks, into, back, down_matrix = lax.optimization_barrier((picks, into, back, down_matrix))
    w_a, w_b, a, b = fetch(
        (down_matrix, down_matrix, a, b),
        ((0, cut, half - cut, 4), (0, half, rest, 7), (1, 0, extent, 1), (1, 0, b.shape[1], 1)),
        "fetch",
    )
    h1a, h2a, h0b, w_a, w_b, a, b = lax.optimization_barrier((h1a, h2a, h0b, w_a, w_b, a, b))
    h3a = hop(h2a, perm=pairs)
    h2b = hop(h0b, perm=twos)
    h1b = hop(h0b, perm=pairs)
    h3b = hop(h2b, perm=pairs)

    base_a, low_a = first_half(picks, (h0a, h1a, h2a, h3a), down_matrix, w_a, a, cut)
    h1b, h3b, base_a, low_a = lax.optimization_barrier((h1b, h3b, base_a, low_a))
    blocks_b = (h0b, h1b, h2b, h3b)
    low_keep, low_send = second_low(picks, blocks_b, a, low_a)
    low_keep, low_send, h0b = lax.optimization_barrier((low_keep, low_send, h0b))
    low_came = lax.ppermute(low_send, "seq", both)
    base_keep, base_send = second_base(picks, (h0b, h1b, h2b, h3b), w_b, base_a)
    base_came = lax.ppermute(base_send, "seq", both)
    low_keep, low_send = split_sum(low_keep, low_came, "split_low")
    low_came = lax.ppermute(low_send, "tensor", both)
    base_keep, base_send = split_sum(base_keep, base_came, "split_base")
    base_send, low_came = lax.optimization_barrier((base_send, low_came))
    base_came = lax.ppermute(base_send, "tensor", both)
    wide = widen(scalars, low_keep, low_came, into, b, slots, owners)
    deltas = [wide[0]]
    for step in range(1, owners):
        deltas.append(hop(wide[step], perm=[(i, (i + step) % owners) for i in range(owners)]))

    return last(base_keep, base_came, back, deltas)


def body(
    hidden, down_matrix, adapter_first_factors, adapter_second_factors, adapter_index_rows, storage
):
    owners = lax.axis_size("adapter")
    groups = lax.axis_size(("tensor", "seq"))
    block_of_rows = hidden.shape[0]
    slice_width = hidden.shape[1]
    stored_factors = adapter_first_factors.shape[0]
    rank_extent = adapter_first_factors.shape[2]
    adapters = storage.shape[0]
    capacity = max(2, min(block_of_rows // 2, 2 * block_of_rows // owners))
    present_block_list = owners // groups
    own_index = lax.axis_index("adapter")
    part_index = lax.axis_index(("tensor", "seq"))
    id_match = adapter_index_rows[:, None] == jnp.arange(adapters, dtype=jnp.int32)[None, :]
    position = jnp.sum(jnp.where(id_match, storage[None, :], 0), axis=1)
    owner_blocks = (position // stored_factors).reshape(owners, block_of_rows)
    local_blocks = (position % stored_factors).reshape(owners, block_of_rows)
    owner_hits = (
        owner_blocks[:, :, None] == jnp.arange(owners, dtype=jnp.int32)[None, None, :]
    ).astype(jnp.int32)
    slot_rank = jnp.sum(owner_hits * (jnp.cumsum(owner_hits, axis=1) - 1), axis=2)
    slot_of = owner_blocks * capacity + slot_rank
    slot_range = jnp.arange(capacity, dtype=jnp.int32)
    owned = owner_blocks == own_index
    picker = owned[:, None, :] & (slot_rank[:, None, :] == slot_range[None, :, None])
    local_in = jnp.sum(jnp.where(picker, local_blocks[:, None, :], 0), axis=2)
    h_all = lax.all_gather(hidden, "adapter", axis=0, tiled=True)
    partial_total = lax.psum_scatter(
        jnp.dot(h_all, down_matrix, preferred_element_type=jnp.float32),
        ("tensor", "seq"),
        scatter_dimension=0,
        tiled=True,
    )
    my_slots = lax.dynamic_index_in_dim(slot_of, own_index, 0, keepdims=False)
    send_pick = my_slots[None, :] == jnp.arange(owners * capacity, dtype=jnp.int32)[:, None]
    send_rows = jnp.dot(send_pick.astype(jnp.bfloat16), hidden, preferred_element_type=jnp.float32)
    send_rows = send_rows.astype(jnp.bfloat16).reshape(owners, capacity, slice_width)
    input_rows = lax.all_to_all(send_rows, "adapter", split_axis=0, concat_axis=0, tiled=True)
    product_terms = jnp.einsum(
        "mbw,twk->mbtk", input_rows, adapter_first_factors, preferred_element_type=jnp.float32
    )
    product_terms = product_terms.reshape(
        input_rows.shape[0], input_rows.shape[1], stored_factors * rank_extent
    )
    select_low = (
        local_in[:, :, None] == jnp.arange(stored_factors, dtype=jnp.int32)[None, None, :]
    ).astype(jnp.float32)
    low_part = jnp.sum(
        product_terms.reshape(owners, capacity, stored_factors, rank_extent)
        * select_low[:, :, :, None],
        axis=2,
    )
    low_rank = lax.psum(low_part, ("tensor", "seq")).astype(jnp.bfloat16)
    owned_lowrank_part = lax.dynamic_slice_in_dim(
        low_rank, part_index * present_block_list, present_block_list, 0
    )
    mine_local = lax.dynamic_slice_in_dim(
        local_in, part_index * present_block_list, present_block_list, 0
    )
    widened_rows = jnp.einsum(
        "jwf,sfe->jwse",
        owned_lowrank_part,
        adapter_second_factors,
        preferred_element_type=jnp.float32,
    )
    select_out = (
        mine_local[:, :, None] == jnp.arange(stored_factors, dtype=jnp.int32)[None, None, :]
    ).astype(jnp.float32)
    delta_rows = jnp.sum(widened_rows * select_out[:, :, :, None], axis=2).astype(jnp.bfloat16)
    returned_rows = lax.all_to_all(delta_rows, "adapter", split_axis=2, concat_axis=1, tiled=True)
    my_targets = lax.dynamic_slice_in_dim(
        slot_of, part_index * present_block_list, present_block_list, 0
    )
    target_pick = (
        my_targets[:, :, None] == jnp.arange(owners * capacity, dtype=jnp.int32)[None, None, :]
    ).astype(jnp.bfloat16)
    adapter_delta_rows = jnp.einsum(
        "prs,psd->prd", target_pick, returned_rows, preferred_element_type=jnp.float32
    )
    adapter_delta_rows = adapter_delta_rows.reshape(
        present_block_list * block_of_rows, returned_rows.shape[2]
    )
    return (partial_total + adapter_delta_rows).astype(jnp.bfloat16)


def solution(mesh):
    placed = (
        P(("groups", "adapter"), ("tensor", "seq")),
        P(("tensor", "seq"), "adapter"),
        P("adapter", ("tensor", "seq"), None),
        P("adapter", None, None),
        P("groups"),
        P("groups"),
    )
    small = mesh.shape["adapter"] == 4 and mesh.shape["tensor"] == 2 and mesh.shape["seq"] == 2
    return jax.shard_map(
        small_body if small else body,
        mesh=mesh,
        in_specs=placed,
        out_specs=P(("groups", "tensor", "seq"), "adapter"),
        check_vma=False,
    )
```

```python
import functools

import jax
import jax.numpy as jnp
from jax import lax
from jax.experimental import pallas as pl
from jax.experimental.pallas import tpu as pltpu
from jax.sharding import PartitionSpec as P

F32 = jnp.float32
BF16 = jnp.bfloat16
MIB = 1024 * 1024
VMEM = pl.BlockSpec(memory_space=pltpu.VMEM)
SMEM = pl.BlockSpec(memory_space=pltpu.SMEM)
HBM = pl.BlockSpec(memory_space=pltpu.HBM)
COLUMNS = 512
FETCH_MIB = 27
SHARE = 8


def params(limit):
    return pltpu.CompilerParams(vmem_limit_bytes=limit * MIB)


def cost(flops, moved):
    return pl.CostEstimate(flops=int(flops), bytes_accessed=int(moved), transcendentals=0)


def fetch_kernel(*refs, pieces):
    count = len(pieces)
    sources, targets, sems = refs[:count], refs[count : 2 * count], refs[2 * count]
    copies = []
    for source, target, (axis, start, length, cuts) in zip(sources, targets, pieces):
        step = length // cuts
        for cut in range(cuts):
            if axis == 0:
                from_ref = source.at[pl.ds(start + cut * step, step)]
                to_ref = target.at[pl.ds(cut * step, step)]
            else:
                from_ref = source.at[:, pl.ds(start + cut * step, step)]
                to_ref = target.at[:, pl.ds(cut * step, step)]
            copies.append(pltpu.make_async_copy(from_ref, to_ref, sems.at[len(copies)]))
    for copy in copies:
        copy.start()
    for copy in copies:
        copy.wait()


def fetch(arrays, pieces, name):
    shapes = []
    for array, (axis, _, length, _) in zip(arrays, pieces):
        shape = list(array.shape)
        shape[axis] = length
        shapes.append(pltpu.VMEM(tuple(shape), array.dtype))
    moved = sum(2 * s.shape[0] * s.shape[1] for s in shapes)
    total = sum(piece[3] for piece in pieces)
    return pl.pallas_call(
        functools.partial(fetch_kernel, pieces=pieces),
        in_specs=[HBM] * len(arrays),
        out_specs=[VMEM] * len(arrays),
        out_shape=shapes,
        scratch_shapes=[pltpu.SemaphoreType.DMA((total,))],
        compiler_params=params(FETCH_MIB),
        cost_estimate=cost(0, moved),
        name=name,
    )(*arrays)


def dot_nt(a, b):
    return lax.dot_general(a, b, (((1,), (1,)), ((), ())), preferred_element_type=F32)


def ordered(blocks, skip):
    own = lax.axis_index("adapter")
    near = (lax.axis_index("seq") ^ (own & 1)) == 1
    far = (lax.axis_index("tensor") ^ (own >> 1)) == 1
    depth = blocks[2].shape[1]
    b0, b1 = [block[:, skip : skip + depth] for block in blocks[:2]]
    b2, b3 = [block[...] for block in blocks[2:]]
    k0, k2 = jnp.where(near, b1, b0), jnp.where(near, b3, b2)
    s0, s2 = jnp.where(near, b0, b1), jnp.where(near, b2, b3)
    return jnp.concatenate(
        [
            jnp.where(far, k2, k0),
            jnp.where(far, k0, k2),
            jnp.where(far, s2, s0),
            jnp.where(far, s0, s2),
        ],
        axis=0,
    )


def first_kernel(
    b0, b1, b2, b3, w_far, w_ref, a_ref, base_ref, low_ref, streamed, sems, *, cuts
):
    cut = streamed.shape[0]
    step = cut // cuts
    copies = []
    for index in range(cuts):
        rows = pl.ds(index * step, step)
        copies.append(pltpu.make_async_copy(w_far.at[rows], streamed.at[rows], sems.at[index]))
        copies[-1].start()
    h = ordered((b0, b1, b2, b3), 0)
    depth = h.shape[1]
    low_ref[...] = dot_nt(h, a_ref[:, :depth])
    for start in range(0, w_ref.shape[1], COLUMNS):
        columns = slice(start, start + COLUMNS)
        base_ref[:, columns] = jnp.dot(h[:, cut:], w_ref[:, columns], preferred_element_type=F32)
    for copy in copies:
        copy.wait()
    for start in range(0, w_ref.shape[1], COLUMNS):
        columns = slice(start, start + COLUMNS)
        base_ref[:, columns] += jnp.dot(
            h[:, :cut], streamed[:, columns], preferred_element_type=F32
        )


def first_half(blocks, w_far, w, a, cut):
    rows, extent = blocks[2].shape
    width, low = w.shape[1], a.shape[0]
    cuts = 4
    return pl.pallas_call(
        functools.partial(first_kernel, cuts=cuts),
        in_specs=[VMEM] * 4 + [HBM] + [VMEM] * 2,
        out_specs=[VMEM] * 2,
        out_shape=[
            jax.ShapeDtypeStruct((4 * rows, width), F32),
            jax.ShapeDtypeStruct((4 * rows, low), F32),
        ],
        scratch_shapes=[pltpu.VMEM((cut, width), BF16), pltpu.SemaphoreType.DMA((cuts,))],
        compiler_params=params(20),
        cost_estimate=cost(8 * rows * extent * (width + low), 4 * MIB),
        name="first_half",
    )(*blocks, w_far, w, a)


def low_kernel(b0, b1, b2, b3, a_ref, low_in, keep_ref, send_ref):
    skip = a_ref.shape[1] - b2.shape[1]
    h = ordered((b0, b1, b2, b3), skip)
    total = low_in[...] + dot_nt(h, a_ref[:, skip:])
    rows = keep_ref.shape[0]
    keep_ref[...] = total[:rows]
    send_ref[...] = total[rows:]


def second_low(blocks, a, low_in):
    rows, extent = blocks[2].shape
    low = a.shape[0]
    return pl.pallas_call(
        low_kernel,
        in_specs=[VMEM] * 6,
        out_specs=[VMEM] * 2,
        out_shape=[jax.ShapeDtypeStruct((2 * rows, low), F32)] * 2,
        compiler_params=params(8),
        cost_estimate=cost(8 * rows * extent * low, MIB),
        name="second_low",
    )(*blocks, a, low_in)


def base_kernel(b0, b1, b2, b3, w_ref, base_in, keep_ref, send_ref):
    h = ordered((b0, b1, b2, b3), b0.shape[1] - b2.shape[1])
    rows = keep_ref.shape[0]
    for start in range(0, w_ref.shape[1], COLUMNS):
        columns = slice(start, start + COLUMNS)
        part = jnp.dot(h, w_ref[:, columns], preferred_element_type=F32)
        total = base_in[:, columns] + part
        keep_ref[:, columns] = total[:rows]
        send_ref[:, columns] = total[rows:].astype(BF16)


def second_base(blocks, w, base_in):
    rows, extent = blocks[2].shape
    width = w.shape[1]
    return pl.pallas_call(
        base_kernel,
        in_specs=[VMEM] * 6,
        out_specs=[VMEM] * 2,
        out_shape=[
            jax.ShapeDtypeStruct((2 * rows, width), F32),
            jax.ShapeDtypeStruct((2 * rows, width), BF16),
        ],
        compiler_params=params(12),
        cost_estimate=cost(8 * rows * extent * width, 4 * MIB),
        name="second_base",
    )(*blocks, w, base_in)


def split_kernel(keep_in, came, keep_ref, send_ref):
    rows = keep_ref.shape[0]
    total = keep_in[...] + came[...].astype(F32)
    keep_ref[...] = total[:rows]
    send_ref[...] = total[rows:].astype(send_ref.dtype)


def split_sum(keep, came, name):
    shape = (keep.shape[0] // 2, keep.shape[1])
    return pl.pallas_call(
        split_kernel,
        in_specs=[VMEM] * 2,
        out_specs=[VMEM] * 2,
        out_shape=[jax.ShapeDtypeStruct(shape, F32), jax.ShapeDtypeStruct(shape, came.dtype)],
        compiler_params=params(4),
        cost_estimate=cost(0, MIB),
        name=name,
    )(keep, came)


def plan_kernel(storage, index_ref, into_ref, back_ref, *, stored, slots):
    own = lax.axis_index("adapter")
    part = lax.axis_index("tensor") * 2 + lax.axis_index("seq")
    rows = back_ref.shape[0]
    shape = (rows, index_ref.shape[1])
    spot = lax.broadcasted_iota(jnp.int32, shape, 0) + part * rows
    chosen = lax.broadcasted_iota(jnp.int32, shape, 1) == spot
    index = jnp.sum(jnp.where(chosen, index_ref[...], 0), axis=1, keepdims=True)

    def position(index):
        found = jnp.zeros_like(index)
        for adapter in range(storage.shape[0]):
            found = jnp.where(index == adapter, storage[adapter], found)
        return found

    def owner_of(place):
        owner = jnp.zeros_like(place)
        for step in range(1, 4):
            owner += (place >= step * stored).astype(jnp.int32)
        return owner

    down = lax.broadcasted_iota(jnp.int32, (rows, rows), 0)
    across = lax.broadcasted_iota(jnp.int32, (rows, rows), 1)

    def turned(column):
        return jnp.sum(jnp.where(down == across, column, 0), axis=0, keepdims=True)

    place_column = position(index)
    owner_column = owner_of(place_column)
    owner_row = turned(owner_column)
    local_row = turned(place_column - owner_column * stored)
    same = owner_column == owner_row
    rank_row = jnp.sum((same & (down < across)).astype(jnp.int32), axis=0, keepdims=True)
    rank_column = jnp.sum((same & (across < down)).astype(jnp.int32), axis=1, keepdims=True)
    slot = lax.broadcasted_iota(jnp.int32, (slots, rows), 0)
    here = (owner_row == own) & (rank_row == slot)
    for index in range(stored):
        taken = here & (local_row == index)
        into_ref[index] = jnp.where(taken, 1.0, 0.0).astype(BF16)
    lane = lax.broadcasted_iota(jnp.int32, (rows, 4 * slots), 1)
    hops = lax.rem(own + 4 - owner_column, 4)
    back_ref[...] = jnp.where(lane == hops * slots + rank_column, 1.0, 0.0).astype(BF16)


def plan(storage, index, rows, stored, slots):
    return pl.pallas_call(
        functools.partial(plan_kernel, stored=stored, slots=slots),
        in_specs=[SMEM, VMEM],
        out_specs=[VMEM] * 2,
        out_shape=[
            jax.ShapeDtypeStruct((stored, slots, rows), BF16),
            jax.ShapeDtypeStruct((rows, 4 * slots), BF16),
        ],
        compiler_params=params(2),
        cost_estimate=cost(0, MIB),
        name="plan",
    )(storage, index[None, :])


def widen_kernel(low_a, low_b, into_ref, b_ref, *outs):
    low = (low_a[...] + low_b[...]).astype(BF16)
    stored = into_ref.shape[0]
    rank_extent = low.shape[1] // stored
    terms = []
    for index in range(stored):
        part = low[:, index * rank_extent : (index + 1) * rank_extent]
        terms.append(jnp.dot(into_ref[index], part, preferred_element_type=F32).astype(BF16))
    packed = jnp.concatenate(terms, axis=1)
    width = outs[0].shape[1]
    for step, out in enumerate(outs):
        start = pl.multiple_of(lax.rem(lax.axis_index("adapter") + step, len(outs)) * width, width)
        columns = b_ref[:, pl.ds(start, width)]
        out[...] = jnp.dot(packed, columns, preferred_element_type=F32).astype(BF16)


def widen(low_a, low_b, into, b, slots, owners):
    width = b.shape[1] // owners
    return pl.pallas_call(
        widen_kernel,
        in_specs=[VMEM] * 4,
        out_specs=[VMEM] * owners,
        out_shape=[jax.ShapeDtypeStruct((slots, width), BF16)] * owners,
        compiler_params=params(6),
        cost_estimate=cost(0, MIB),
        name="widen",
    )(low_a, low_b, into, b)


def last_kernel(keep, came, back, d0, d1, d2, d3, out_ref):
    deltas = jnp.concatenate([d[...] for d in (d0, d1, d2, d3)], axis=0)
    delta = jnp.dot(back[...], deltas, preferred_element_type=F32)
    out_ref[...] = (keep[...] + came[...].astype(F32) + delta).astype(out_ref.dtype)


def last(keep, came, back, deltas):
    return pl.pallas_call(
        last_kernel,
        in_specs=[VMEM] * 7,
        out_specs=VMEM,
        out_shape=jax.ShapeDtypeStruct(keep.shape, BF16),
        compiler_params=params(4),
        cost_estimate=cost(0, MIB),
        name="last",
    )(keep, came, back, *deltas)


def small_body(
    hidden, down_matrix, adapter_first_factors, adapter_second_factors, adapter_index_rows, storage
):
    owners = 4
    rows, extent = hidden.shape
    stored, _, rank_extent = adapter_first_factors.shape
    slots = max(2, min(rows // 2, 2 * rows // owners))
    half = 256 * (extent * SHARE // (256 * 16))
    cut = half // 2
    rest = extent - half

    a = jnp.swapaxes(adapter_first_factors, 1, 2).reshape(stored * rank_extent, extent)
    b = adapter_second_factors.reshape(stored * rank_extent, -1)
    pairs = [(0, 1), (1, 0), (2, 3), (3, 2)]
    twos = [(0, 2), (2, 0), (1, 3), (3, 1)]
    both = [(0, 1), (1, 0)]
    hop = functools.partial(lax.ppermute, axis_name="adapter")

    barrier = lax.optimization_barrier
    h0 = hidden
    h1 = hop(h0, perm=pairs)
    h0a, h0b = hidden[:, :half], hidden[:, half:]
    h2a = hop(h0a, perm=twos)
    (w_b,) = fetch((down_matrix,), ((0, half, rest, 7),), "fetch_b")
    w_b, h0b, a, b = barrier((w_b, h0b, a, b))
    h2b = hop(h0b, perm=twos)
    w_a, a, b = fetch(
        (down_matrix, a, b),
        ((0, cut, half - cut, 4), (1, 0, extent, 1), (1, 0, b.shape[1], 1)),
        "fetch_a",
    )
    h2a, w_a, a, b, adapter_index_rows = barrier((h2a, w_a, a, b, adapter_index_rows))
    h3a = hop(h2a, perm=pairs)
    into, back = plan(storage, adapter_index_rows, rows, stored, slots)
    h2b, into, back = barrier((h2b, into, back))
    h3b = hop(h2b, perm=pairs)

    base_a, low_a = first_half((h0, h1, h2a, h3a), down_matrix, w_a, a, cut)
    h3b, base_a, low_a = barrier((h3b, base_a, low_a))
    blocks_b = (h0, h1, h2b, h3b)
    low_keep, low_send = second_low(blocks_b, a, low_a)
    low_came = lax.ppermute(low_send, "seq", both)
    low_keep, low_send = split_sum(low_keep, low_came, "split_low")
    low_came = lax.ppermute(low_send, "tensor", both)
    w_b, low_keep = barrier((w_b, low_keep))
    base_keep, base_send = second_base(blocks_b, w_b, base_a)
    base_send, low_came = barrier((base_send, low_came))
    base_came = lax.ppermute(base_send, "seq", both)
    wide = widen(low_keep, low_came, into, b, slots, owners)
    deltas = [wide[0]]
    for step in range(1, owners):
        deltas.append(hop(wide[step], perm=[(i, (i + step) % owners) for i in range(owners)]))
    base_keep, base_send = split_sum(base_keep, base_came, "split_base")
    base_came = lax.ppermute(base_send, "tensor", both)
    return last(base_keep, base_came, back, deltas)


def body(
    hidden, down_matrix, adapter_first_factors, adapter_second_factors, adapter_index_rows, storage
):
    owners = lax.axis_size("adapter")
    groups = lax.axis_size(("tensor", "seq"))
    block_of_rows = hidden.shape[0]
    slice_width = hidden.shape[1]
    stored_factors = adapter_first_factors.shape[0]
    rank_extent = adapter_first_factors.shape[2]
    adapters = storage.shape[0]
    capacity = max(2, min(block_of_rows // 2, 2 * block_of_rows // owners))
    present_block_list = owners // groups
    own_index = lax.axis_index("adapter")
    part_index = lax.axis_index(("tensor", "seq"))
    id_match = adapter_index_rows[:, None] == jnp.arange(adapters, dtype=jnp.int32)[None, :]
    position = jnp.sum(jnp.where(id_match, storage[None, :], 0), axis=1)
    owner_blocks = (position // stored_factors).reshape(owners, block_of_rows)
    local_blocks = (position % stored_factors).reshape(owners, block_of_rows)
    owner_hits = (
        owner_blocks[:, :, None] == jnp.arange(owners, dtype=jnp.int32)[None, None, :]
    ).astype(jnp.int32)
    slot_rank = jnp.sum(owner_hits * (jnp.cumsum(owner_hits, axis=1) - 1), axis=2)
    slot_of = owner_blocks * capacity + slot_rank
    slot_range = jnp.arange(capacity, dtype=jnp.int32)
    owned = owner_blocks == own_index
    picker = owned[:, None, :] & (slot_rank[:, None, :] == slot_range[None, :, None])
    local_in = jnp.sum(jnp.where(picker, local_blocks[:, None, :], 0), axis=2)
    h_all = lax.all_gather(hidden, "adapter", axis=0, tiled=True)
    partial_total = lax.psum_scatter(
        jnp.dot(h_all, down_matrix, preferred_element_type=jnp.float32),
        ("tensor", "seq"),
        scatter_dimension=0,
        tiled=True,
    )
    my_slots = lax.dynamic_index_in_dim(slot_of, own_index, 0, keepdims=False)
    send_pick = my_slots[None, :] == jnp.arange(owners * capacity, dtype=jnp.int32)[:, None]
    send_rows = jnp.dot(send_pick.astype(jnp.bfloat16), hidden, preferred_element_type=jnp.float32)
    send_rows = send_rows.astype(jnp.bfloat16).reshape(owners, capacity, slice_width)
    input_rows = lax.all_to_all(send_rows, "adapter", split_axis=0, concat_axis=0, tiled=True)
    product_terms = jnp.einsum(
        "mbw,twk->mbtk", input_rows, adapter_first_factors, preferred_element_type=jnp.float32
    )
    product_terms = product_terms.reshape(
        input_rows.shape[0], input_rows.shape[1], stored_factors * rank_extent
    )
    select_low = (
        local_in[:, :, None] == jnp.arange(stored_factors, dtype=jnp.int32)[None, None, :]
    ).astype(jnp.float32)
    low_part = jnp.sum(
        product_terms.reshape(owners, capacity, stored_factors, rank_extent)
        * select_low[:, :, :, None],
        axis=2,
    )
    low_rank = lax.psum(low_part, ("tensor", "seq")).astype(jnp.bfloat16)
    owned_lowrank_part = lax.dynamic_slice_in_dim(
        low_rank, part_index * present_block_list, present_block_list, 0
    )
    mine_local = lax.dynamic_slice_in_dim(
        local_in, part_index * present_block_list, present_block_list, 0
    )
    widened_rows = jnp.einsum(
        "jwf,sfe->jwse",
        owned_lowrank_part,
        adapter_second_factors,
        preferred_element_type=jnp.float32,
    )
    select_out = (
        mine_local[:, :, None] == jnp.arange(stored_factors, dtype=jnp.int32)[None, None, :]
    ).astype(jnp.float32)
    delta_rows = jnp.sum(widened_rows * select_out[:, :, :, None], axis=2).astype(jnp.bfloat16)
    returned_rows = lax.all_to_all(delta_rows, "adapter", split_axis=2, concat_axis=1, tiled=True)
    my_targets = lax.dynamic_slice_in_dim(
        slot_of, part_index * present_block_list, present_block_list, 0
    )
    target_pick = (
        my_targets[:, :, None] == jnp.arange(owners * capacity, dtype=jnp.int32)[None, None, :]
    ).astype(jnp.bfloat16)
    adapter_delta_rows = jnp.einsum(
        "prs,psd->prd", target_pick, returned_rows, preferred_element_type=jnp.float32
    )
    adapter_delta_rows = adapter_delta_rows.reshape(
        present_block_list * block_of_rows, returned_rows.shape[2]
    )
    return (partial_total + adapter_delta_rows).astype(jnp.bfloat16)


def solution(mesh):
    placed = (
        P(("groups", "adapter"), ("tensor", "seq")),
        P(("tensor", "seq"), "adapter"),
        P("adapter", ("tensor", "seq"), None),
        P("adapter", None, None),
        P("groups"),
        P("groups"),
    )
    small = mesh.shape["adapter"] == 4 and mesh.shape["tensor"] == 2 and mesh.shape["seq"] == 2
    return jax.shard_map(
        small_body if small else body,
        mesh=mesh,
        in_specs=placed,
        out_specs=P(("groups", "tensor", "seq"), "adapter"),
        check_vma=False,
    )
```

```python
import functools

import jax
import jax.numpy as jnp
from jax import lax
from jax.experimental import pallas as pl
from jax.experimental.pallas import tpu as pltpu
from jax.sharding import PartitionSpec as P

F32 = jnp.float32
BF16 = jnp.bfloat16
MIB = 1024 * 1024
VMEM = pl.BlockSpec(memory_space=pltpu.VMEM)
SMEM = pl.BlockSpec(memory_space=pltpu.SMEM)
HBM = pl.BlockSpec(memory_space=pltpu.HBM)
COLUMNS = 512
FETCH_MIB = 27
SHARE = 8
CUT = 14
ADD_FLOPS = 8e9


def params(limit):
    return pltpu.CompilerParams(vmem_limit_bytes=limit * MIB)


def cost(flops, moved):
    return pl.CostEstimate(flops=int(flops), bytes_accessed=int(moved), transcendentals=0)


def fetch_kernel(*refs, pieces):
    count = len(pieces)
    sources, targets, sems = refs[:count], refs[count : 2 * count], refs[2 * count]
    copies = []
    for source, target, (axis, start, length, cuts) in zip(sources, targets, pieces):
        step = length // cuts
        for cut in range(cuts):
            if axis == 0:
                from_ref = source.at[pl.ds(start + cut * step, step)]
                to_ref = target.at[pl.ds(cut * step, step)]
            else:
                from_ref = source.at[:, pl.ds(start + cut * step, step)]
                to_ref = target.at[:, pl.ds(cut * step, step)]
            copies.append(pltpu.make_async_copy(from_ref, to_ref, sems.at[len(copies)]))
    for copy in copies:
        copy.start()
    for copy in copies:
        copy.wait()


def fetch(arrays, pieces, name):
    shapes = []
    for array, (axis, _, length, _) in zip(arrays, pieces):
        shape = list(array.shape)
        shape[axis] = length
        shapes.append(pltpu.VMEM(tuple(shape), array.dtype))
    moved = sum(2 * s.shape[0] * s.shape[1] for s in shapes)
    total = sum(piece[3] for piece in pieces)
    return pl.pallas_call(
        functools.partial(fetch_kernel, pieces=pieces),
        in_specs=[HBM] * len(arrays),
        out_specs=[VMEM] * len(arrays),
        out_shape=shapes,
        scratch_shapes=[pltpu.SemaphoreType.DMA((total,))],
        compiler_params=params(FETCH_MIB),
        cost_estimate=cost(0, moved),
        name=name,
    )(*arrays)


def dot_nt(a, b):
    return lax.dot_general(a, b, (((1,), (1,)), ((), ())), preferred_element_type=F32)


def ordered(blocks, skip):
    own = lax.axis_index("adapter")
    near = (lax.axis_index("seq") ^ (own & 1)) == 1
    far = (lax.axis_index("tensor") ^ (own >> 1)) == 1
    depth = blocks[2].shape[1]
    b0, b1 = [block[:, skip : skip + depth] for block in blocks[:2]]
    b2, b3 = [block[...] for block in blocks[2:]]
    k0, k2 = jnp.where(near, b1, b0), jnp.where(near, b3, b2)
    s0, s2 = jnp.where(near, b0, b1), jnp.where(near, b2, b3)
    return jnp.concatenate(
        [
            jnp.where(far, k2, k0),
            jnp.where(far, k0, k2),
            jnp.where(far, s2, s0),
            jnp.where(far, s0, s2),
        ],
        axis=0,
    )


def first_kernel(
    b0, b1, b2, b3, w_far, w_ref, a_ref, base_ref, low_ref, streamed, sems, *, cuts
):
    cut = streamed.shape[0]
    step = cut // cuts
    copies = []
    for index in range(cuts):
        rows = pl.ds(index * step, step)
        copies.append(pltpu.make_async_copy(w_far.at[rows], streamed.at[rows], sems.at[index]))
        copies[-1].start()
    h = ordered((b0, b1, b2, b3), 0)
    depth = h.shape[1]
    low_ref[...] = dot_nt(h, a_ref[:, :depth])
    for start in range(0, w_ref.shape[1], COLUMNS):
        columns = slice(start, start + COLUMNS)
        base_ref[:, columns] = jnp.dot(h[:, cut:], w_ref[:, columns], preferred_element_type=F32)
    for copy in copies:
        copy.wait()
    for start in range(0, w_ref.shape[1], COLUMNS):
        columns = slice(start, start + COLUMNS)
        base_ref[:, columns] += jnp.dot(
            h[:, :cut], streamed[:, columns], preferred_element_type=F32
        )


def first_half(blocks, w_far, w, a, cut):
    rows, extent = blocks[2].shape
    width, low = w.shape[1], a.shape[0]
    cuts = 4
    return pl.pallas_call(
        functools.partial(first_kernel, cuts=cuts),
        in_specs=[VMEM] * 4 + [HBM] + [VMEM] * 2,
        out_specs=[VMEM] * 2,
        out_shape=[
            jax.ShapeDtypeStruct((4 * rows, width), F32),
            jax.ShapeDtypeStruct((4 * rows, low), F32),
        ],
        scratch_shapes=[pltpu.VMEM((cut, width), BF16), pltpu.SemaphoreType.DMA((cuts,))],
        compiler_params=params(20),
        cost_estimate=cost(8 * rows * extent * (width + low), 4 * MIB),
        name="first_half",
    )(*blocks, w_far, w, a)


def low_kernel(b0, b1, b2, b3, a_ref, low_in, keep_ref, send_ref):
    skip = a_ref.shape[1] - b2.shape[1]
    h = ordered((b0, b1, b2, b3), skip)
    total = low_in[...] + dot_nt(h, a_ref[:, skip:])
    rows = keep_ref.shape[0]
    keep_ref[...] = total[:rows]
    send_ref[...] = total[rows:]


def second_low(blocks, a, low_in):
    rows, extent = blocks[2].shape
    low = a.shape[0]
    return pl.pallas_call(
        low_kernel,
        in_specs=[VMEM] * 6,
        out_specs=[VMEM] * 2,
        out_shape=[jax.ShapeDtypeStruct((2 * rows, low), F32)] * 2,
        compiler_params=params(8),
        cost_estimate=cost(8 * rows * extent * low, MIB),
        name="second_low",
    )(*blocks, a, low_in)


def base_kernel(b0, b1, b2, b3, w_ref, base_in, keep_ref, send_ref):
    h = ordered((b0, b1, b2, b3), b0.shape[1] - b2.shape[1])
    rows = keep_ref.shape[0]
    for start in range(0, w_ref.shape[1], COLUMNS):
        columns = slice(start, start + COLUMNS)
        part = jnp.dot(h, w_ref[:, columns], preferred_element_type=F32)
        total = base_in[:, columns] + part
        keep_ref[:, columns] = total[:rows]
        send_ref[:, columns] = total[rows:].astype(BF16)


def second_base(blocks, w, base_in):
    rows, extent = blocks[2].shape
    width = w.shape[1]
    return pl.pallas_call(
        base_kernel,
        in_specs=[VMEM] * 6,
        out_specs=[VMEM] * 2,
        out_shape=[
            jax.ShapeDtypeStruct((2 * rows, width), F32),
            jax.ShapeDtypeStruct((2 * rows, width), BF16),
        ],
        compiler_params=params(12),
        cost_estimate=cost(8 * rows * extent * width, 4 * MIB),
        name="second_base",
    )(*blocks, w, base_in)


def split_kernel(keep_in, came, keep_ref, send_ref):
    rows = keep_ref.shape[0]
    total = keep_in[...] + came[...].astype(F32)
    keep_ref[...] = total[:rows]
    send_ref[...] = total[rows:].astype(send_ref.dtype)


def split_sum(keep, came, name):
    shape = (keep.shape[0] // 2, keep.shape[1])
    return pl.pallas_call(
        split_kernel,
        in_specs=[VMEM] * 2,
        out_specs=[VMEM] * 2,
        out_shape=[jax.ShapeDtypeStruct(shape, F32), jax.ShapeDtypeStruct(shape, came.dtype)],
        compiler_params=params(4),
        cost_estimate=cost(0, MIB),
        name=name,
    )(keep, came)


def plan_kernel(storage, index_ref, into_ref, back_ref, *, stored, slots):
    own = lax.axis_index("adapter")
    part = lax.axis_index("tensor") * 2 + lax.axis_index("seq")
    rows = back_ref.shape[0]
    shape = (rows, index_ref.shape[1])
    spot = lax.broadcasted_iota(jnp.int32, shape, 0) + part * rows
    chosen = lax.broadcasted_iota(jnp.int32, shape, 1) == spot
    index = jnp.sum(jnp.where(chosen, index_ref[...], 0), axis=1, keepdims=True)

    def position(index):
        found = jnp.zeros_like(index)
        for adapter in range(storage.shape[0]):
            found = jnp.where(index == adapter, storage[adapter], found)
        return found

    def owner_of(place):
        owner = jnp.zeros_like(place)
        for step in range(1, 4):
            owner += (place >= step * stored).astype(jnp.int32)
        return owner

    down = lax.broadcasted_iota(jnp.int32, (rows, rows), 0)
    across = lax.broadcasted_iota(jnp.int32, (rows, rows), 1)

    def turned(column):
        return jnp.sum(jnp.where(down == across, column, 0), axis=0, keepdims=True)

    place_column = position(index)
    owner_column = owner_of(place_column)
    owner_row = turned(owner_column)
    local_row = turned(place_column - owner_column * stored)
    same = owner_column == owner_row
    rank_row = jnp.sum((same & (down < across)).astype(jnp.int32), axis=0, keepdims=True)
    rank_column = jnp.sum((same & (across < down)).astype(jnp.int32), axis=1, keepdims=True)
    slot = lax.broadcasted_iota(jnp.int32, (slots, rows), 0)
    here = (owner_row == own) & (rank_row == slot)
    for index in range(stored):
        taken = here & (local_row == index)
        into_ref[index] = jnp.where(taken, 1.0, 0.0).astype(BF16)
    lane = lax.broadcasted_iota(jnp.int32, (rows, 4 * slots), 1)
    hops = lax.rem(own + 4 - owner_column, 4)
    back_ref[...] = jnp.where(lane == hops * slots + rank_column, 1.0, 0.0).astype(BF16)


def plan(storage, index, rows, stored, slots):
    return pl.pallas_call(
        functools.partial(plan_kernel, stored=stored, slots=slots),
        in_specs=[SMEM, VMEM],
        out_specs=[VMEM] * 2,
        out_shape=[
            jax.ShapeDtypeStruct((stored, slots, rows), BF16),
            jax.ShapeDtypeStruct((rows, 4 * slots), BF16),
        ],
        compiler_params=params(2),
        cost_estimate=cost(0, MIB),
        name="plan",
    )(storage, index[None, :])


def widen_kernel(low_a, low_b, into_ref, b_ref, *outs):
    low = (low_a[...] + low_b[...]).astype(BF16)
    stored = into_ref.shape[0]
    rank_extent = low.shape[1] // stored
    terms = []
    for index in range(stored):
        part = low[:, index * rank_extent : (index + 1) * rank_extent]
        terms.append(jnp.dot(into_ref[index], part, preferred_element_type=F32).astype(BF16))
    packed = jnp.concatenate(terms, axis=1)
    width = outs[0].shape[1]
    for step, out in enumerate(outs):
        start = pl.multiple_of(lax.rem(lax.axis_index("adapter") + step, len(outs)) * width, width)
        columns = b_ref[:, pl.ds(start, width)]
        out[...] = jnp.dot(packed, columns, preferred_element_type=F32).astype(BF16)


def widen(low_a, low_b, into, b, slots, owners):
    width = b.shape[1] // owners
    return pl.pallas_call(
        widen_kernel,
        in_specs=[VMEM] * 4,
        out_specs=[VMEM] * owners,
        out_shape=[jax.ShapeDtypeStruct((slots, width), BF16)] * owners,
        compiler_params=params(6),
        cost_estimate=cost(0, MIB),
        name="widen",
    )(low_a, low_b, into, b)


def add_kernel(keep, back, d0, d1, d2, d3, out_ref):
    deltas = jnp.concatenate([d[...] for d in (d0, d1, d2, d3)], axis=0)
    out_ref[...] = keep[...] + jnp.dot(back[...], deltas, preferred_element_type=F32)


def add_rows(keep, back, deltas):
    return pl.pallas_call(
        add_kernel,
        in_specs=[VMEM] * 6,
        out_specs=VMEM,
        out_shape=jax.ShapeDtypeStruct(keep.shape, F32),
        compiler_params=params(4),
        cost_estimate=cost(ADD_FLOPS, MIB),
        name="add_rows",
    )(keep, back, *deltas)


def last_kernel(keep, came, out_ref):
    out_ref[...] = (keep[...] + came[...].astype(F32)).astype(out_ref.dtype)


def last(keep, came):
    return pl.pallas_call(
        last_kernel,
        in_specs=[VMEM] * 2,
        out_specs=VMEM,
        out_shape=jax.ShapeDtypeStruct(keep.shape, BF16),
        compiler_params=params(4),
        cost_estimate=cost(0, MIB),
        name="last",
    )(keep, came)


def small_body(
    hidden, down_matrix, adapter_first_factors, adapter_second_factors, adapter_index_rows, storage
):
    owners = 4
    rows, extent = hidden.shape
    stored, _, rank_extent = adapter_first_factors.shape
    slots = max(2, min(rows // 2, 2 * rows // owners))
    half = 256 * (extent * SHARE // (256 * 16))
    cut = 128 * (extent * CUT // (128 * 56))
    rest = extent - half

    a = jnp.swapaxes(adapter_first_factors, 1, 2).reshape(stored * rank_extent, extent)
    b = adapter_second_factors.reshape(stored * rank_extent, -1)
    pairs = [(0, 1), (1, 0), (2, 3), (3, 2)]
    twos = [(0, 2), (2, 0), (1, 3), (3, 1)]
    both = [(0, 1), (1, 0)]
    hop = functools.partial(lax.ppermute, axis_name="adapter")

    barrier = lax.optimization_barrier
    h0 = hidden
    h1 = hop(h0, perm=pairs)
    h0a, h0b = hidden[:, :half], hidden[:, half:]
    h2a = hop(h0a, perm=twos)
    (w_b,) = fetch((down_matrix,), ((0, half, rest, 7),), "fetch_b")
    w_b, h0b, a, b = barrier((w_b, h0b, a, b))
    h2b = hop(h0b, perm=twos)
    w_a, a, b = fetch(
        (down_matrix, a, b),
        ((0, cut, half - cut, 4), (1, 0, extent, 1), (1, 0, b.shape[1], 1)),
        "fetch_a",
    )
    h2a, w_a, a, b, adapter_index_rows = barrier((h2a, w_a, a, b, adapter_index_rows))
    h3a = hop(h2a, perm=pairs)
    into, back = plan(storage, adapter_index_rows, rows, stored, slots)
    h2b, into, back = barrier((h2b, into, back))
    h3b = hop(h2b, perm=pairs)

    base_a, low_a = first_half((h0, h1, h2a, h3a), down_matrix, w_a, a, cut)
    h3b, base_a, low_a = barrier((h3b, base_a, low_a))
    blocks_b = (h0, h1, h2b, h3b)
    low_keep, low_send = second_low(blocks_b, a, low_a)
    low_came = lax.ppermute(low_send, "seq", both)
    low_keep, low_send = split_sum(low_keep, low_came, "split_low")
    low_came = lax.ppermute(low_send, "tensor", both)
    w_b, low_keep = barrier((w_b, low_keep))
    base_keep, base_send = second_base(blocks_b, w_b, base_a)
    base_keep, low_came = barrier((base_keep, low_came))
    wide = widen(low_keep, low_came, into, b, slots, owners)
    base_send, wide = barrier((base_send, wide))
    base_came = lax.ppermute(base_send, "seq", both)
    deltas = [wide[0]]
    for step in range(1, owners):
        deltas.append(hop(wide[step], perm=[(i, (i + step) % owners) for i in range(owners)]))
    base_keep, base_send = split_sum(base_keep, base_came, "split_base")
    base_came = lax.ppermute(base_send, "tensor", both)
    return last(add_rows(base_keep, back, deltas), base_came)


def body(
    hidden, down_matrix, adapter_first_factors, adapter_second_factors, adapter_index_rows, storage
):
    owners = lax.axis_size("adapter")
    groups = lax.axis_size(("tensor", "seq"))
    block_of_rows = hidden.shape[0]
    slice_width = hidden.shape[1]
    stored_factors = adapter_first_factors.shape[0]
    rank_extent = adapter_first_factors.shape[2]
    adapters = storage.shape[0]
    capacity = max(2, min(block_of_rows // 2, 2 * block_of_rows // owners))
    present_block_list = owners // groups
    own_index = lax.axis_index("adapter")
    part_index = lax.axis_index(("tensor", "seq"))
    id_match = adapter_index_rows[:, None] == jnp.arange(adapters, dtype=jnp.int32)[None, :]
    position = jnp.sum(jnp.where(id_match, storage[None, :], 0), axis=1)
    owner_blocks = (position // stored_factors).reshape(owners, block_of_rows)
    local_blocks = (position % stored_factors).reshape(owners, block_of_rows)
    owner_hits = (
        owner_blocks[:, :, None] == jnp.arange(owners, dtype=jnp.int32)[None, None, :]
    ).astype(jnp.int32)
    slot_rank = jnp.sum(owner_hits * (jnp.cumsum(owner_hits, axis=1) - 1), axis=2)
    slot_of = owner_blocks * capacity + slot_rank
    slot_range = jnp.arange(capacity, dtype=jnp.int32)
    owned = owner_blocks == own_index
    picker = owned[:, None, :] & (slot_rank[:, None, :] == slot_range[None, :, None])
    local_in = jnp.sum(jnp.where(picker, local_blocks[:, None, :], 0), axis=2)
    h_all = lax.all_gather(hidden, "adapter", axis=0, tiled=True)
    partial_total = lax.psum_scatter(
        jnp.dot(h_all, down_matrix, preferred_element_type=jnp.float32),
        ("tensor", "seq"),
        scatter_dimension=0,
        tiled=True,
    )
    my_slots = lax.dynamic_index_in_dim(slot_of, own_index, 0, keepdims=False)
    send_pick = my_slots[None, :] == jnp.arange(owners * capacity, dtype=jnp.int32)[:, None]
    send_rows = jnp.dot(send_pick.astype(jnp.bfloat16), hidden, preferred_element_type=jnp.float32)
    send_rows = send_rows.astype(jnp.bfloat16).reshape(owners, capacity, slice_width)
    input_rows = lax.all_to_all(send_rows, "adapter", split_axis=0, concat_axis=0, tiled=True)
    product_terms = jnp.einsum(
        "mbw,twk->mbtk", input_rows, adapter_first_factors, preferred_element_type=jnp.float32
    )
    product_terms = product_terms.reshape(
        input_rows.shape[0], input_rows.shape[1], stored_factors * rank_extent
    )
    select_low = (
        local_in[:, :, None] == jnp.arange(stored_factors, dtype=jnp.int32)[None, None, :]
    ).astype(jnp.float32)
    low_part = jnp.sum(
        product_terms.reshape(owners, capacity, stored_factors, rank_extent)
        * select_low[:, :, :, None],
        axis=2,
    )
    low_rank = lax.psum(low_part, ("tensor", "seq")).astype(jnp.bfloat16)
    owned_lowrank_part = lax.dynamic_slice_in_dim(
        low_rank, part_index * present_block_list, present_block_list, 0
    )
    mine_local = lax.dynamic_slice_in_dim(
        local_in, part_index * present_block_list, present_block_list, 0
    )
    widened_rows = jnp.einsum(
        "jwf,sfe->jwse",
        owned_lowrank_part,
        adapter_second_factors,
        preferred_element_type=jnp.float32,
    )
    select_out = (
        mine_local[:, :, None] == jnp.arange(stored_factors, dtype=jnp.int32)[None, None, :]
    ).astype(jnp.float32)
    delta_rows = jnp.sum(widened_rows * select_out[:, :, :, None], axis=2).astype(jnp.bfloat16)
    returned_rows = lax.all_to_all(delta_rows, "adapter", split_axis=2, concat_axis=1, tiled=True)
    my_targets = lax.dynamic_slice_in_dim(
        slot_of, part_index * present_block_list, present_block_list, 0
    )
    target_pick = (
        my_targets[:, :, None] == jnp.arange(owners * capacity, dtype=jnp.int32)[None, None, :]
    ).astype(jnp.bfloat16)
    adapter_delta_rows = jnp.einsum(
        "prs,psd->prd", target_pick, returned_rows, preferred_element_type=jnp.float32
    )
    adapter_delta_rows = adapter_delta_rows.reshape(
        present_block_list * block_of_rows, returned_rows.shape[2]
    )
    return (partial_total + adapter_delta_rows).astype(jnp.bfloat16)


def solution(mesh):
    placed = (
        P(("groups", "adapter"), ("tensor", "seq")),
        P(("tensor", "seq"), "adapter"),
        P("adapter", ("tensor", "seq"), None),
        P("adapter", None, None),
        P("groups"),
        P("groups"),
    )
    small = mesh.shape["adapter"] == 4 and mesh.shape["tensor"] == 2 and mesh.shape["seq"] == 2
    return jax.shard_map(
        small_body if small else body,
        mesh=mesh,
        in_specs=placed,
        out_specs=P(("groups", "tensor", "seq"), "adapter"),
        check_vma=False,
    )
```

```python
import functools

import jax
import jax.numpy as jnp
from jax import lax
from jax.experimental import pallas as pl
from jax.experimental.pallas import tpu as pltpu
from jax.sharding import PartitionSpec as P

F32 = jnp.float32
BF16 = jnp.bfloat16
MIB = 1024 * 1024
VMEM = pl.BlockSpec(memory_space=pltpu.VMEM)
SMEM = pl.BlockSpec(memory_space=pltpu.SMEM)
HBM = pl.BlockSpec(memory_space=pltpu.HBM)
COLUMNS = 512
FETCH_MIB = 27
SHARE = 8
FETCH_A = 0.01
FETCH_B = 1.0
CUT = 7
ADD_FLOPS = 8e9


def params(limit):
    return pltpu.CompilerParams(vmem_limit_bytes=limit * MIB)


def cost(flops, moved):
    return pl.CostEstimate(flops=int(flops), bytes_accessed=int(moved), transcendentals=0)


def fetch_kernel(*refs, pieces):
    count = len(pieces)
    sources, targets, sems = refs[:count], refs[count : 2 * count], refs[2 * count]
    copies = []
    for source, target, (axis, start, length, cuts) in zip(sources, targets, pieces):
        step = length // cuts
        for cut in range(cuts):
            if axis == 0:
                from_ref = source.at[pl.ds(start + cut * step, step)]
                to_ref = target.at[pl.ds(cut * step, step)]
            else:
                from_ref = source.at[:, pl.ds(start + cut * step, step)]
                to_ref = target.at[:, pl.ds(cut * step, step)]
            copies.append(pltpu.make_async_copy(from_ref, to_ref, sems.at[len(copies)]))
    for copy in copies:
        copy.start()
    for copy in copies:
        copy.wait()


def fetch(arrays, pieces, name, weight=1.0):
    shapes = []
    for array, (axis, _, length, _) in zip(arrays, pieces):
        shape = list(array.shape)
        shape[axis] = length
        shapes.append(pltpu.VMEM(tuple(shape), array.dtype))
    moved = sum(2 * s.shape[0] * s.shape[1] for s in shapes)
    total = sum(piece[3] for piece in pieces)
    return pl.pallas_call(
        functools.partial(fetch_kernel, pieces=pieces),
        in_specs=[HBM] * len(arrays),
        out_specs=[VMEM] * len(arrays),
        out_shape=shapes,
        scratch_shapes=[pltpu.SemaphoreType.DMA((total,))],
        compiler_params=params(FETCH_MIB),
        cost_estimate=cost(0, weight * moved),
        name=name,
    )(*arrays)


def dot_nt(a, b):
    return lax.dot_general(a, b, (((1,), (1,)), ((), ())), preferred_element_type=F32)


def ordered(blocks, skip):
    own = lax.axis_index("adapter")
    near = (lax.axis_index("seq") ^ (own & 1)) == 1
    far = (lax.axis_index("tensor") ^ (own >> 1)) == 1
    depth = blocks[2].shape[1]
    b0, b1 = [block[:, skip : skip + depth] for block in blocks[:2]]
    b2, b3 = [block[...] for block in blocks[2:]]
    k0, k2 = jnp.where(near, b1, b0), jnp.where(near, b3, b2)
    s0, s2 = jnp.where(near, b0, b1), jnp.where(near, b2, b3)
    return jnp.concatenate(
        [
            jnp.where(far, k2, k0),
            jnp.where(far, k0, k2),
            jnp.where(far, s2, s0),
            jnp.where(far, s0, s2),
        ],
        axis=0,
    )


def first_kernel(
    b0, b1, b2, b3, w_far, w_ref, a_ref, base_ref, low_ref, streamed, sems, *, cuts
):
    cut = streamed.shape[0]
    step = cut // cuts
    copies = []
    for index in range(cuts):
        rows = pl.ds(index * step, step)
        copies.append(pltpu.make_async_copy(w_far.at[rows], streamed.at[rows], sems.at[index]))
        copies[-1].start()
    h = ordered((b0, b1, b2, b3), 0)
    depth = h.shape[1]
    low_ref[...] = dot_nt(h, a_ref[:, :depth])
    for start in range(0, w_ref.shape[1], COLUMNS):
        columns = slice(start, start + COLUMNS)
        base_ref[:, columns] = jnp.dot(h[:, cut:], w_ref[:, columns], preferred_element_type=F32)
    for copy in copies:
        copy.wait()
    for start in range(0, w_ref.shape[1], COLUMNS):
        columns = slice(start, start + COLUMNS)
        base_ref[:, columns] += jnp.dot(
            h[:, :cut], streamed[:, columns], preferred_element_type=F32
        )


def first_half(blocks, w_far, w, a, cut):
    rows, extent = blocks[2].shape
    width, low = w.shape[1], a.shape[0]
    cuts = 4
    return pl.pallas_call(
        functools.partial(first_kernel, cuts=cuts),
        in_specs=[VMEM] * 4 + [HBM] + [VMEM] * 2,
        out_specs=[VMEM] * 2,
        out_shape=[
            jax.ShapeDtypeStruct((4 * rows, width), F32),
            jax.ShapeDtypeStruct((4 * rows, low), F32),
        ],
        scratch_shapes=[pltpu.VMEM((cut, width), BF16), pltpu.SemaphoreType.DMA((cuts,))],
        compiler_params=params(20),
        cost_estimate=cost(8 * rows * extent * (width + low), 4 * MIB),
        name="first_half",
    )(*blocks, w_far, w, a)


def low_kernel(b0, b1, b2, b3, a_ref, low_in, keep_ref, send_ref):
    skip = a_ref.shape[1] - b2.shape[1]
    h = ordered((b0, b1, b2, b3), skip)
    total = low_in[...] + dot_nt(h, a_ref[:, skip:])
    rows = keep_ref.shape[0]
    keep_ref[...] = total[:rows]
    send_ref[...] = total[rows:]


def second_low(blocks, a, low_in):
    rows, extent = blocks[2].shape
    low = a.shape[0]
    return pl.pallas_call(
        low_kernel,
        in_specs=[VMEM] * 6,
        out_specs=[VMEM] * 2,
        out_shape=[jax.ShapeDtypeStruct((2 * rows, low), F32)] * 2,
        compiler_params=params(8),
        cost_estimate=cost(8 * rows * extent * low, MIB),
        name="second_low",
    )(*blocks, a, low_in)


def base_kernel(b0, b1, b2, b3, w_ref, base_in, keep_ref, send_ref):
    h = ordered((b0, b1, b2, b3), b0.shape[1] - b2.shape[1])
    rows = keep_ref.shape[0]
    for start in range(0, w_ref.shape[1], COLUMNS):
        columns = slice(start, start + COLUMNS)
        part = jnp.dot(h, w_ref[:, columns], preferred_element_type=F32)
        total = base_in[:, columns] + part
        keep_ref[:, columns] = total[:rows]
        send_ref[:, columns] = total[rows:].astype(BF16)


def second_base(blocks, w, base_in):
    rows, extent = blocks[2].shape
    width = w.shape[1]
    return pl.pallas_call(
        base_kernel,
        in_specs=[VMEM] * 6,
        out_specs=[VMEM] * 2,
        out_shape=[
            jax.ShapeDtypeStruct((2 * rows, width), F32),
            jax.ShapeDtypeStruct((2 * rows, width), BF16),
        ],
        compiler_params=params(12),
        cost_estimate=cost(8 * rows * extent * width, 4 * MIB),
        name="second_base",
    )(*blocks, w, base_in)


def split_kernel(keep_in, came, keep_ref, send_ref):
    rows = keep_ref.shape[0]
    total = keep_in[...] + came[...].astype(F32)
    keep_ref[...] = total[:rows]
    send_ref[...] = total[rows:].astype(send_ref.dtype)


def split_sum(keep, came, name):
    shape = (keep.shape[0] // 2, keep.shape[1])
    return pl.pallas_call(
        split_kernel,
        in_specs=[VMEM] * 2,
        out_specs=[VMEM] * 2,
        out_shape=[jax.ShapeDtypeStruct(shape, F32), jax.ShapeDtypeStruct(shape, came.dtype)],
        compiler_params=params(4),
        cost_estimate=cost(0, MIB),
        name=name,
    )(keep, came)


def plan_kernel(storage, index_ref, into_ref, back_ref, *, stored, slots):
    own = lax.axis_index("adapter")
    part = lax.axis_index("tensor") * 2 + lax.axis_index("seq")
    rows = back_ref.shape[0]
    shape = (rows, index_ref.shape[1])
    spot = lax.broadcasted_iota(jnp.int32, shape, 0) + part * rows
    chosen = lax.broadcasted_iota(jnp.int32, shape, 1) == spot
    index = jnp.sum(jnp.where(chosen, index_ref[...], 0), axis=1, keepdims=True)

    def position(index):
        found = jnp.zeros_like(index)
        for adapter in range(storage.shape[0]):
            found = jnp.where(index == adapter, storage[adapter], found)
        return found

    def owner_of(place):
        owner = jnp.zeros_like(place)
        for step in range(1, 4):
            owner += (place >= step * stored).astype(jnp.int32)
        return owner

    down = lax.broadcasted_iota(jnp.int32, (rows, rows), 0)
    across = lax.broadcasted_iota(jnp.int32, (rows, rows), 1)

    def turned(column):
        return jnp.sum(jnp.where(down == across, column, 0), axis=0, keepdims=True)

    place_column = position(index)
    owner_column = owner_of(place_column)
    owner_row = turned(owner_column)
    local_row = turned(place_column - owner_column * stored)
    same = owner_column == owner_row
    rank_row = jnp.sum((same & (down < across)).astype(jnp.int32), axis=0, keepdims=True)
    rank_column = jnp.sum((same & (across < down)).astype(jnp.int32), axis=1, keepdims=True)
    slot = lax.broadcasted_iota(jnp.int32, (slots, rows), 0)
    here = (owner_row == own) & (rank_row == slot)
    for index in range(stored):
        taken = here & (local_row == index)
        into_ref[index] = jnp.where(taken, 1.0, 0.0).astype(BF16)
    lane = lax.broadcasted_iota(jnp.int32, (rows, 4 * slots), 1)
    hops = lax.rem(own + 4 - owner_column, 4)
    back_ref[...] = jnp.where(lane == hops * slots + rank_column, 1.0, 0.0).astype(BF16)


def plan(storage, index, rows, stored, slots):
    return pl.pallas_call(
        functools.partial(plan_kernel, stored=stored, slots=slots),
        in_specs=[SMEM, VMEM],
        out_specs=[VMEM] * 2,
        out_shape=[
            jax.ShapeDtypeStruct((stored, slots, rows), BF16),
            jax.ShapeDtypeStruct((rows, 4 * slots), BF16),
        ],
        compiler_params=params(2),
        cost_estimate=cost(0, MIB),
        name="plan",
    )(storage, index[None, :])


def widen_kernel(low_a, low_b, into_ref, b_ref, *outs):
    low = (low_a[...] + low_b[...]).astype(BF16)
    stored = into_ref.shape[0]
    rank_extent = low.shape[1] // stored
    terms = []
    for index in range(stored):
        part = low[:, index * rank_extent : (index + 1) * rank_extent]
        terms.append(jnp.dot(into_ref[index], part, preferred_element_type=F32).astype(BF16))
    packed = jnp.concatenate(terms, axis=1)
    width = outs[0].shape[1]
    for step, out in enumerate(outs):
        start = pl.multiple_of(lax.rem(lax.axis_index("adapter") + step, len(outs)) * width, width)
        columns = b_ref[:, pl.ds(start, width)]
        out[...] = jnp.dot(packed, columns, preferred_element_type=F32).astype(BF16)


def widen(low_a, low_b, into, b, slots, owners):
    width = b.shape[1] // owners
    return pl.pallas_call(
        widen_kernel,
        in_specs=[VMEM] * 4,
        out_specs=[VMEM] * owners,
        out_shape=[jax.ShapeDtypeStruct((slots, width), BF16)] * owners,
        compiler_params=params(6),
        cost_estimate=cost(0, MIB),
        name="widen",
    )(low_a, low_b, into, b)


def add_kernel(keep, back, d0, d1, d3, d2, out_ref):
    deltas = jnp.concatenate([d[...] for d in (d0, d1, d2, d3)], axis=0)
    out_ref[...] = keep[...] + jnp.dot(back[...], deltas, preferred_element_type=F32)


def add_rows(keep, back, deltas):
    return pl.pallas_call(
        add_kernel,
        in_specs=[VMEM] * 6,
        out_specs=VMEM,
        out_shape=jax.ShapeDtypeStruct(keep.shape, F32),
        compiler_params=params(4),
        cost_estimate=cost(ADD_FLOPS, MIB),
        name="add_rows",
    )(keep, back, deltas[0], deltas[1], deltas[3], deltas[2])


def last_kernel(keep, came, out_ref):
    out_ref[...] = (keep[...] + came[...].astype(F32)).astype(out_ref.dtype)


def last(keep, came):
    return pl.pallas_call(
        last_kernel,
        in_specs=[VMEM] * 2,
        out_specs=VMEM,
        out_shape=jax.ShapeDtypeStruct(keep.shape, BF16),
        compiler_params=params(4),
        cost_estimate=cost(0, MIB),
        name="last",
    )(keep, came)


def small_body(
    hidden, down_matrix, adapter_first_factors, adapter_second_factors, adapter_index_rows, storage
):
    owners = 4
    rows, extent = hidden.shape
    stored, _, rank_extent = adapter_first_factors.shape
    slots = max(2, min(rows // 2, 2 * rows // owners))
    half = 128 * (extent * SHARE // (128 * 16))
    cut = 128 * (extent * CUT // (128 * 56))
    rest = extent - half

    a = jnp.swapaxes(adapter_first_factors, 1, 2).reshape(stored * rank_extent, extent)
    b = adapter_second_factors.reshape(stored * rank_extent, -1)
    pairs = [(0, 1), (1, 0), (2, 3), (3, 2)]
    twos = [(0, 2), (2, 0), (1, 3), (3, 1)]
    both = [(0, 1), (1, 0)]
    hop = functools.partial(lax.ppermute, axis_name="adapter")

    barrier = lax.optimization_barrier
    h0 = hidden
    h1 = hop(h0, perm=pairs)
    h0a = hidden[:, :half]
    h2a = hop(h0a, perm=twos)
    (w_b,) = fetch((down_matrix,), ((0, half, rest, 7),), "fetch_b", FETCH_B)
    w_b, hidden, down_matrix = barrier((w_b, hidden, down_matrix))
    (h0b,) = fetch((hidden,), ((1, half, rest, 1),), "half_b")
    h2b = hop(h0b, perm=twos)
    (w_a,) = fetch(
        (down_matrix,),
        ((0, cut, half - cut, 4),),
        "fetch_a",
        FETCH_A,
    )
    h2a, w_a, adapter_index_rows = barrier((h2a, w_a, adapter_index_rows))
    h3a = hop(h2a, perm=pairs)
    into, back = plan(storage, adapter_index_rows, rows, stored, slots)
    h2b, into, back = barrier((h2b, into, back))
    h3b = hop(h2b, perm=pairs)

    base_a, low_a = first_half((h0, h1, h2a, h3a), down_matrix, w_a, a, cut)
    h3b, base_a, low_a = barrier((h3b, base_a, low_a))
    blocks_b = (h0, h1, h2b, h3b)
    low_keep, low_send = second_low(blocks_b, a, low_a)
    low_came = lax.ppermute(low_send, "seq", both)
    low_keep, low_send = split_sum(low_keep, low_came, "split_low")
    low_came = lax.ppermute(low_send, "tensor", both)
    w_b, low_keep = barrier((w_b, low_keep))
    base_keep, base_send = second_base(blocks_b, w_b, base_a)
    base_keep, low_came = barrier((base_keep, low_came))
    wide = widen(low_keep, low_came, into, b, slots, owners)
    base_send, wide = barrier((base_send, wide))
    base_came = lax.ppermute(base_send, "seq", both)
    deltas = {0: wide[0]}
    for step in (1, 2, 3):
        deltas[step] = hop(wide[step], perm=[(i, (i + step) % owners) for i in range(owners)])
    deltas = [deltas[step] for step in range(owners)]
    base_keep, base_send = split_sum(base_keep, base_came, "split_base")
    base_came = lax.ppermute(base_send, "tensor", both)
    return last(add_rows(base_keep, back, deltas), base_came)


def body(
    hidden, down_matrix, adapter_first_factors, adapter_second_factors, adapter_index_rows, storage
):
    owners = lax.axis_size("adapter")
    groups = lax.axis_size(("tensor", "seq"))
    block_of_rows = hidden.shape[0]
    slice_width = hidden.shape[1]
    stored_factors = adapter_first_factors.shape[0]
    rank_extent = adapter_first_factors.shape[2]
    adapters = storage.shape[0]
    capacity = max(2, min(block_of_rows // 2, 2 * block_of_rows // owners))
    present_block_list = owners // groups
    own_index = lax.axis_index("adapter")
    part_index = lax.axis_index(("tensor", "seq"))
    id_match = adapter_index_rows[:, None] == jnp.arange(adapters, dtype=jnp.int32)[None, :]
    position = jnp.sum(jnp.where(id_match, storage[None, :], 0), axis=1)
    owner_blocks = (position // stored_factors).reshape(owners, block_of_rows)
    local_blocks = (position % stored_factors).reshape(owners, block_of_rows)
    owner_hits = (
        owner_blocks[:, :, None] == jnp.arange(owners, dtype=jnp.int32)[None, None, :]
    ).astype(jnp.int32)
    slot_rank = jnp.sum(owner_hits * (jnp.cumsum(owner_hits, axis=1) - 1), axis=2)
    slot_of = owner_blocks * capacity + slot_rank
    slot_range = jnp.arange(capacity, dtype=jnp.int32)
    owned = owner_blocks == own_index
    picker = owned[:, None, :] & (slot_rank[:, None, :] == slot_range[None, :, None])
    local_in = jnp.sum(jnp.where(picker, local_blocks[:, None, :], 0), axis=2)
    h_all = lax.all_gather(hidden, "adapter", axis=0, tiled=True)
    partial_total = lax.psum_scatter(
        jnp.dot(h_all, down_matrix, preferred_element_type=jnp.float32),
        ("tensor", "seq"),
        scatter_dimension=0,
        tiled=True,
    )
    my_slots = lax.dynamic_index_in_dim(slot_of, own_index, 0, keepdims=False)
    send_pick = my_slots[None, :] == jnp.arange(owners * capacity, dtype=jnp.int32)[:, None]
    send_rows = jnp.dot(send_pick.astype(jnp.bfloat16), hidden, preferred_element_type=jnp.float32)
    send_rows = send_rows.astype(jnp.bfloat16).reshape(owners, capacity, slice_width)
    input_rows = lax.all_to_all(send_rows, "adapter", split_axis=0, concat_axis=0, tiled=True)
    product_terms = jnp.einsum(
        "mbw,twk->mbtk", input_rows, adapter_first_factors, preferred_element_type=jnp.float32
    )
    product_terms = product_terms.reshape(
        input_rows.shape[0], input_rows.shape[1], stored_factors * rank_extent
    )
    select_low = (
        local_in[:, :, None] == jnp.arange(stored_factors, dtype=jnp.int32)[None, None, :]
    ).astype(jnp.float32)
    low_part = jnp.sum(
        product_terms.reshape(owners, capacity, stored_factors, rank_extent)
        * select_low[:, :, :, None],
        axis=2,
    )
    low_rank = lax.psum(low_part, ("tensor", "seq")).astype(jnp.bfloat16)
    owned_lowrank_part = lax.dynamic_slice_in_dim(
        low_rank, part_index * present_block_list, present_block_list, 0
    )
    mine_local = lax.dynamic_slice_in_dim(
        local_in, part_index * present_block_list, present_block_list, 0
    )
    widened_rows = jnp.einsum(
        "jwf,sfe->jwse",
        owned_lowrank_part,
        adapter_second_factors,
        preferred_element_type=jnp.float32,
    )
    select_out = (
        mine_local[:, :, None] == jnp.arange(stored_factors, dtype=jnp.int32)[None, None, :]
    ).astype(jnp.float32)
    delta_rows = jnp.sum(widened_rows * select_out[:, :, :, None], axis=2).astype(jnp.bfloat16)
    returned_rows = lax.all_to_all(delta_rows, "adapter", split_axis=2, concat_axis=1, tiled=True)
    my_targets = lax.dynamic_slice_in_dim(
        slot_of, part_index * present_block_list, present_block_list, 0
    )
    target_pick = (
        my_targets[:, :, None] == jnp.arange(owners * capacity, dtype=jnp.int32)[None, None, :]
    ).astype(jnp.bfloat16)
    adapter_delta_rows = jnp.einsum(
        "prs,psd->prd", target_pick, returned_rows, preferred_element_type=jnp.float32
    )
    adapter_delta_rows = adapter_delta_rows.reshape(
        present_block_list * block_of_rows, returned_rows.shape[2]
    )
    return (partial_total + adapter_delta_rows).astype(jnp.bfloat16)


def solution(mesh):
    placed = (
        P(("groups", "adapter"), ("tensor", "seq")),
        P(("tensor", "seq"), "adapter"),
        P("adapter", ("tensor", "seq"), None),
        P("adapter", None, None),
        P("groups"),
        P("groups"),
    )
    small = mesh.shape["adapter"] == 4 and mesh.shape["tensor"] == 2 and mesh.shape["seq"] == 2
    return jax.shard_map(
        small_body if small else body,
        mesh=mesh,
        in_specs=placed,
        out_specs=P(("groups", "tensor", "seq"), "adapter"),
        check_vma=False,
    )
```

```python
import functools

import jax
import jax.numpy as jnp
from jax import lax
from jax.experimental import pallas as pl
from jax.experimental.pallas import tpu as pltpu
from jax.sharding import PartitionSpec as P

F32 = jnp.float32
BF16 = jnp.bfloat16
MIB = 1024 * 1024
VMEM = pl.BlockSpec(memory_space=pltpu.VMEM)
SMEM = pl.BlockSpec(memory_space=pltpu.SMEM)
HBM = pl.BlockSpec(memory_space=pltpu.HBM)
COLUMNS = 512
FETCH_MIB = 27
SHARE = 8
MIDDLE = 12
FETCH_A = 0.01
FETCH_B = 1.0
CUT = 7
ADD_FLOPS = 8e9


def params(limit):
    return pltpu.CompilerParams(vmem_limit_bytes=limit * MIB)


def cost(flops, moved):
    return pl.CostEstimate(flops=int(flops), bytes_accessed=int(moved), transcendentals=0)


def fetch_kernel(*refs, pieces):
    count = len(pieces)
    sources, targets, sems = refs[:count], refs[count : 2 * count], refs[2 * count]
    copies = []
    for source, target, (axis, start, length, cuts) in zip(sources, targets, pieces):
        step = length // cuts
        for cut in range(cuts):
            if axis == 0:
                from_ref = source.at[pl.ds(start + cut * step, step)]
                to_ref = target.at[pl.ds(cut * step, step)]
            else:
                from_ref = source.at[:, pl.ds(start + cut * step, step)]
                to_ref = target.at[:, pl.ds(cut * step, step)]
            copies.append(pltpu.make_async_copy(from_ref, to_ref, sems.at[len(copies)]))
    for copy in copies:
        copy.start()
    for copy in copies:
        copy.wait()


def fetch(arrays, pieces, name, weight=1.0):
    shapes = []
    for array, (axis, _, length, _) in zip(arrays, pieces):
        shape = list(array.shape)
        shape[axis] = length
        shapes.append(pltpu.VMEM(tuple(shape), array.dtype))
    moved = sum(2 * s.shape[0] * s.shape[1] for s in shapes)
    total = sum(piece[3] for piece in pieces)
    return pl.pallas_call(
        functools.partial(fetch_kernel, pieces=pieces),
        in_specs=[HBM] * len(arrays),
        out_specs=[VMEM] * len(arrays),
        out_shape=shapes,
        scratch_shapes=[pltpu.SemaphoreType.DMA((total,))],
        compiler_params=params(FETCH_MIB),
        cost_estimate=cost(0, weight * moved),
        name=name,
    )(*arrays)


def dot_nt(a, b):
    return lax.dot_general(a, b, (((1,), (1,)), ((), ())), preferred_element_type=F32)


def ordered(blocks, skip):
    own = lax.axis_index("adapter")
    near = (lax.axis_index("seq") ^ (own & 1)) == 1
    far = (lax.axis_index("tensor") ^ (own >> 1)) == 1
    depth = blocks[2].shape[1]
    b0, b1, b2, b3 = [
        block[...] if block.shape[1] == depth else block[:, skip : skip + depth]
        for block in blocks
    ]
    k0, k2 = jnp.where(near, b1, b0), jnp.where(near, b3, b2)
    s0, s2 = jnp.where(near, b0, b1), jnp.where(near, b2, b3)
    return jnp.concatenate(
        [
            jnp.where(far, k2, k0),
            jnp.where(far, k0, k2),
            jnp.where(far, s2, s0),
            jnp.where(far, s0, s2),
        ],
        axis=0,
    )


def first_kernel(
    b0, b1, b2, b3, w_far, w_ref, a_ref, base_ref, low_ref, streamed, sems, *, cuts, stop
):
    cut = streamed.shape[0]
    step = cut // cuts
    copies = []
    for index in range(cuts):
        rows = pl.ds(index * step, step)
        copies.append(pltpu.make_async_copy(w_far.at[rows], streamed.at[rows], sems.at[index]))
        copies[-1].start()
    h = ordered((b0, b1, b2, b3), 0)
    depth = h.shape[1]
    low_ref[...] = dot_nt(h, a_ref[:, :depth])
    for start in range(0, w_ref.shape[1], COLUMNS):
        columns = slice(start, start + COLUMNS)
        base_ref[:, columns] = jnp.dot(
            h[:, cut:stop], w_ref[: stop - cut, columns], preferred_element_type=F32
        )
    for copy in copies:
        copy.wait()
    for start in range(0, w_ref.shape[1], COLUMNS):
        columns = slice(start, start + COLUMNS)
        base_ref[:, columns] += jnp.dot(
            h[:, :cut], streamed[:, columns], preferred_element_type=F32
        )


def first_half(blocks, w_far, w, a, cut, stop):
    rows, extent = blocks[2].shape
    width, low = w.shape[1], a.shape[0]
    cuts = 4
    return pl.pallas_call(
        functools.partial(first_kernel, cuts=cuts, stop=stop),
        in_specs=[VMEM] * 4 + [HBM] + [VMEM] * 2,
        out_specs=[VMEM] * 2,
        out_shape=[
            jax.ShapeDtypeStruct((4 * rows, width), F32),
            jax.ShapeDtypeStruct((4 * rows, low), F32),
        ],
        scratch_shapes=[pltpu.VMEM((cut, width), BF16), pltpu.SemaphoreType.DMA((cuts,))],
        compiler_params=params(20),
        cost_estimate=cost(8 * rows * extent * (width + low), 4 * MIB),
        name="first_half",
    )(*blocks, w_far, w, a)


def low_kernel(b0, b1, b2, b3, a_ref, low_in, keep_ref, send_ref):
    skip = a_ref.shape[1] - b2.shape[1]
    h = ordered((b0, b1, b2, b3), skip)
    total = low_in[...] + dot_nt(h, a_ref[:, skip:])
    rows = keep_ref.shape[0]
    keep_ref[...] = total[:rows]
    send_ref[...] = total[rows:]


def second_low(blocks, a, low_in):
    rows, extent = blocks[2].shape
    low = a.shape[0]
    return pl.pallas_call(
        low_kernel,
        in_specs=[VMEM] * 6,
        out_specs=[VMEM] * 2,
        out_shape=[jax.ShapeDtypeStruct((2 * rows, low), F32)] * 2,
        compiler_params=params(8),
        cost_estimate=cost(8 * rows * extent * low, MIB),
        name="second_low",
    )(*blocks, a, low_in)


def middle_kernel(b0, b1, b2, b3, w_ref, base_in, base_ref, *, depth):
    h = ordered((b0, b1, b2, b3), 0)
    taken, held = h.shape[1] - depth, w_ref.shape[0] - depth
    for start in range(0, w_ref.shape[1], COLUMNS):
        columns = slice(start, start + COLUMNS)
        part = jnp.dot(h[:, taken:], w_ref[held:, columns], preferred_element_type=F32)
        base_ref[:, columns] = base_in[:, columns] + part


def middle_base(blocks, w, base_in, depth):
    rows = blocks[2].shape[0]
    return pl.pallas_call(
        functools.partial(middle_kernel, depth=depth),
        in_specs=[VMEM] * 6,
        out_specs=VMEM,
        out_shape=jax.ShapeDtypeStruct(base_in.shape, F32),
        compiler_params=params(8),
        cost_estimate=cost(8 * rows * depth * w.shape[1], 4 * MIB),
        name="middle_base",
    )(*blocks, w, base_in)


def base_kernel(b0, b1, b2, b3, w_ref, base_in, keep_ref, send_ref):
    h = ordered((b0, b1, b2, b3), b1.shape[1] - b2.shape[1])
    rows = keep_ref.shape[0]
    for start in range(0, w_ref.shape[1], COLUMNS):
        columns = slice(start, start + COLUMNS)
        part = jnp.dot(h, w_ref[:, columns], preferred_element_type=F32)
        total = base_in[:, columns] + part
        keep_ref[:, columns] = total[:rows]
        send_ref[:, columns] = total[rows:].astype(BF16)


def second_base(blocks, w, base_in):
    rows, extent = blocks[2].shape
    width = w.shape[1]
    return pl.pallas_call(
        base_kernel,
        in_specs=[VMEM] * 6,
        out_specs=[VMEM] * 2,
        out_shape=[
            jax.ShapeDtypeStruct((2 * rows, width), F32),
            jax.ShapeDtypeStruct((2 * rows, width), BF16),
        ],
        compiler_params=params(12),
        cost_estimate=cost(8 * rows * extent * width, 4 * MIB),
        name="second_base",
    )(*blocks, w, base_in)


def split_kernel(keep_in, came, keep_ref, send_ref):
    rows = keep_ref.shape[0]
    total = keep_in[...] + came[...].astype(F32)
    keep_ref[...] = total[:rows]
    send_ref[...] = total[rows:].astype(send_ref.dtype)


def split_sum(keep, came, name):
    shape = (keep.shape[0] // 2, keep.shape[1])
    return pl.pallas_call(
        split_kernel,
        in_specs=[VMEM] * 2,
        out_specs=[VMEM] * 2,
        out_shape=[jax.ShapeDtypeStruct(shape, F32), jax.ShapeDtypeStruct(shape, came.dtype)],
        compiler_params=params(4),
        cost_estimate=cost(0, MIB),
        name=name,
    )(keep, came)


def plan_kernel(storage, index_ref, into_ref, back_ref, *, stored, slots):
    own = lax.axis_index("adapter")
    part = lax.axis_index("tensor") * 2 + lax.axis_index("seq")
    rows = back_ref.shape[0]
    shape = (rows, index_ref.shape[1])
    spot = lax.broadcasted_iota(jnp.int32, shape, 0) + part * rows
    chosen = lax.broadcasted_iota(jnp.int32, shape, 1) == spot
    index = jnp.sum(jnp.where(chosen, index_ref[...], 0), axis=1, keepdims=True)

    def position(index):
        found = jnp.zeros_like(index)
        for adapter in range(storage.shape[0]):
            found = jnp.where(index == adapter, storage[adapter], found)
        return found

    def owner_of(place):
        owner = jnp.zeros_like(place)
        for step in range(1, 4):
            owner += (place >= step * stored).astype(jnp.int32)
        return owner

    down = lax.broadcasted_iota(jnp.int32, (rows, rows), 0)
    across = lax.broadcasted_iota(jnp.int32, (rows, rows), 1)

    def turned(column):
        return jnp.sum(jnp.where(down == across, column, 0), axis=0, keepdims=True)

    place_column = position(index)
    owner_column = owner_of(place_column)
    owner_row = turned(owner_column)
    local_row = turned(place_column - owner_column * stored)
    same = owner_column == owner_row
    rank_row = jnp.sum((same & (down < across)).astype(jnp.int32), axis=0, keepdims=True)
    rank_column = jnp.sum((same & (across < down)).astype(jnp.int32), axis=1, keepdims=True)
    slot = lax.broadcasted_iota(jnp.int32, (slots, rows), 0)
    here = (owner_row == own) & (rank_row == slot)
    for index in range(stored):
        taken = here & (local_row == index)
        into_ref[index] = jnp.where(taken, 1.0, 0.0).astype(BF16)
    lane = lax.broadcasted_iota(jnp.int32, (rows, 4 * slots), 1)
    hops = owner_column ^ own
    back_ref[...] = jnp.where(lane == hops * slots + rank_column, 1.0, 0.0).astype(BF16)


def plan(storage, index, rows, stored, slots):
    return pl.pallas_call(
        functools.partial(plan_kernel, stored=stored, slots=slots),
        in_specs=[SMEM, VMEM],
        out_specs=[VMEM] * 2,
        out_shape=[
            jax.ShapeDtypeStruct((stored, slots, rows), BF16),
            jax.ShapeDtypeStruct((rows, 4 * slots), BF16),
        ],
        compiler_params=params(2),
        cost_estimate=cost(0, MIB),
        name="plan",
    )(storage, index[None, :])


def widen_kernel(low_a, low_b, into_ref, b_ref, *outs):
    low = (low_a[...] + low_b[...]).astype(BF16)
    stored = into_ref.shape[0]
    rank_extent = low.shape[1] // stored
    terms = []
    for index in range(stored):
        part = low[:, index * rank_extent : (index + 1) * rank_extent]
        terms.append(jnp.dot(into_ref[index], part, preferred_element_type=F32).astype(BF16))
    packed = jnp.concatenate(terms, axis=1)
    width = outs[0].shape[1]
    for step, out in enumerate(outs):
        start = pl.multiple_of((lax.axis_index("adapter") ^ step) * width, width)
        columns = b_ref[:, pl.ds(start, width)]
        out[...] = jnp.dot(packed, columns, preferred_element_type=F32).astype(BF16)


def widen(low_a, low_b, into, b, slots, owners):
    width = b.shape[1] // owners
    return pl.pallas_call(
        widen_kernel,
        in_specs=[VMEM] * 4,
        out_specs=[VMEM] * owners,
        out_shape=[jax.ShapeDtypeStruct((slots, width), BF16)] * owners,
        compiler_params=params(6),
        cost_estimate=cost(0, MIB),
        name="widen",
    )(low_a, low_b, into, b)


def add_kernel(keep, back, d0, d3, d1, d2, out_ref):
    deltas = jnp.concatenate([d[...] for d in (d0, d1, d2, d3)], axis=0)
    out_ref[...] = keep[...] + jnp.dot(back[...], deltas, preferred_element_type=F32)


def add_rows(keep, back, deltas):
    return pl.pallas_call(
        add_kernel,
        in_specs=[VMEM] * 6,
        out_specs=VMEM,
        out_shape=jax.ShapeDtypeStruct(keep.shape, F32),
        compiler_params=params(4),
        cost_estimate=cost(ADD_FLOPS, MIB),
        name="add_rows",
    )(keep, back, deltas[0], deltas[3], deltas[1], deltas[2])


def last_kernel(keep, came, out_ref):
    out_ref[...] = (keep[...] + came[...].astype(F32)).astype(out_ref.dtype)


def last(keep, came):
    return pl.pallas_call(
        last_kernel,
        in_specs=[VMEM] * 2,
        out_specs=VMEM,
        out_shape=jax.ShapeDtypeStruct(keep.shape, BF16),
        compiler_params=params(4),
        cost_estimate=cost(0, MIB),
        name="last",
    )(keep, came)


def small_body(
    hidden, down_matrix, adapter_first_factors, adapter_second_factors, adapter_index_rows, storage
):
    owners = 4
    rows, extent = hidden.shape
    stored, _, rank_extent = adapter_first_factors.shape
    slots = max(2, min(rows // 2, 2 * rows // owners))
    half = 128 * (extent * SHARE // (128 * 16))
    cut = 128 * (extent * CUT // (128 * 56))
    middle = 128 * (extent * MIDDLE // (128 * 56))
    rest = extent - half

    a = jnp.swapaxes(adapter_first_factors, 1, 2).reshape(stored * rank_extent, extent)
    b = adapter_second_factors.reshape(stored * rank_extent, -1)
    pairs = [(0, 1), (1, 0), (2, 3), (3, 2)]
    twos = [(0, 2), (2, 0), (1, 3), (3, 1)]
    both = [(0, 1), (1, 0)]
    hop = functools.partial(lax.ppermute, axis_name="adapter")

    barrier = lax.optimization_barrier
    h0 = hidden
    h1 = hop(h0, perm=pairs)
    h0a = hidden[:, :half]
    h2a = hop(h0a, perm=twos)
    (w_b,) = fetch((down_matrix,), ((0, half, rest, 7),), "fetch_b", FETCH_B)
    w_b, hidden, down_matrix = barrier((w_b, hidden, down_matrix))
    (h0b,) = fetch((hidden,), ((1, half, rest, 1),), "half_b")
    h2b = hop(h0b, perm=twos)
    (w_a,) = fetch(
        (down_matrix,),
        ((0, cut, half - cut, 4),),
        "fetch_a",
        FETCH_A,
    )
    h2a, w_a, adapter_index_rows = barrier((h2a, w_a, adapter_index_rows))
    h3a = hop(h2a, perm=pairs)
    into, back = plan(storage, adapter_index_rows, rows, stored, slots)
    h2b, into, back = barrier((h2b, into, back))
    h3b = hop(h2b, perm=pairs)

    blocks_a = (h0, h1, h2a, h3a)
    base_a, low_a = first_half(blocks_a, down_matrix, w_a, a, cut, half - middle)
    h3b, base_a, low_a = barrier((h3b, base_a, low_a))
    blocks_b = (h0, h1, h2b, h3b)
    low_keep, low_send = second_low(blocks_b, a, low_a)
    w_a, low_keep = barrier((w_a, low_keep))
    low_came = lax.ppermute(low_send, "seq", both)
    base_a = middle_base(blocks_a, w_a, base_a, middle)
    low_came, base_a = barrier((low_came, base_a))
    low_keep, low_send = split_sum(low_keep, low_came, "split_low")
    low_came = lax.ppermute(low_send, "tensor", both)
    w_b, low_keep = barrier((w_b, low_keep))
    base_keep, base_send = second_base(blocks_b, w_b, base_a)
    base_keep, low_came = barrier((base_keep, low_came))
    wide = widen(low_keep, low_came, into, b, slots, owners)
    base_send, wide = barrier((base_send, wide))
    base_came = lax.ppermute(base_send, "seq", both)
    deltas = {0: wide[0]}
    for step in (1, 2, 3):
        deltas[step] = hop(wide[step], perm=[(i, i ^ step) for i in range(owners)])
    deltas = [deltas[step] for step in range(owners)]
    base_keep, base_send = split_sum(base_keep, base_came, "split_base")
    base_came = lax.ppermute(base_send, "tensor", both)
    return last(add_rows(base_keep, back, deltas), base_came)


def body(
    hidden, down_matrix, adapter_first_factors, adapter_second_factors, adapter_index_rows, storage
):
    owners = lax.axis_size("adapter")
    groups = lax.axis_size(("tensor", "seq"))
    block_of_rows = hidden.shape[0]
    slice_width = hidden.shape[1]
    stored_factors = adapter_first_factors.shape[0]
    rank_extent = adapter_first_factors.shape[2]
    adapters = storage.shape[0]
    capacity = max(2, min(block_of_rows // 2, 2 * block_of_rows // owners))
    present_block_list = owners // groups
    own_index = lax.axis_index("adapter")
    part_index = lax.axis_index(("tensor", "seq"))
    id_match = adapter_index_rows[:, None] == jnp.arange(adapters, dtype=jnp.int32)[None, :]
    position = jnp.sum(jnp.where(id_match, storage[None, :], 0), axis=1)
    owner_blocks = (position // stored_factors).reshape(owners, block_of_rows)
    local_blocks = (position % stored_factors).reshape(owners, block_of_rows)
    owner_hits = (
        owner_blocks[:, :, None] == jnp.arange(owners, dtype=jnp.int32)[None, None, :]
    ).astype(jnp.int32)
    slot_rank = jnp.sum(owner_hits * (jnp.cumsum(owner_hits, axis=1) - 1), axis=2)
    slot_of = owner_blocks * capacity + slot_rank
    slot_range = jnp.arange(capacity, dtype=jnp.int32)
    owned = owner_blocks == own_index
    picker = owned[:, None, :] & (slot_rank[:, None, :] == slot_range[None, :, None])
    local_in = jnp.sum(jnp.where(picker, local_blocks[:, None, :], 0), axis=2)
    h_all = lax.all_gather(hidden, "adapter", axis=0, tiled=True)
    partial_total = lax.psum_scatter(
        jnp.dot(h_all, down_matrix, preferred_element_type=jnp.float32),
        ("tensor", "seq"),
        scatter_dimension=0,
        tiled=True,
    )
    my_slots = lax.dynamic_index_in_dim(slot_of, own_index, 0, keepdims=False)
    send_pick = my_slots[None, :] == jnp.arange(owners * capacity, dtype=jnp.int32)[:, None]
    send_rows = jnp.dot(send_pick.astype(jnp.bfloat16), hidden, preferred_element_type=jnp.float32)
    send_rows = send_rows.astype(jnp.bfloat16).reshape(owners, capacity, slice_width)
    input_rows = lax.all_to_all(send_rows, "adapter", split_axis=0, concat_axis=0, tiled=True)
    product_terms = jnp.einsum(
        "mbw,twk->mbtk", input_rows, adapter_first_factors, preferred_element_type=jnp.float32
    )
    product_terms = product_terms.reshape(
        input_rows.shape[0], input_rows.shape[1], stored_factors * rank_extent
    )
    select_low = (
        local_in[:, :, None] == jnp.arange(stored_factors, dtype=jnp.int32)[None, None, :]
    ).astype(jnp.float32)
    low_part = jnp.sum(
        product_terms.reshape(owners, capacity, stored_factors, rank_extent)
        * select_low[:, :, :, None],
        axis=2,
    )
    low_rank = lax.psum(low_part, ("tensor", "seq")).astype(jnp.bfloat16)
    owned_lowrank_part = lax.dynamic_slice_in_dim(
        low_rank, part_index * present_block_list, present_block_list, 0
    )
    mine_local = lax.dynamic_slice_in_dim(
        local_in, part_index * present_block_list, present_block_list, 0
    )
    widened_rows = jnp.einsum(
        "jwf,sfe->jwse",
        owned_lowrank_part,
        adapter_second_factors,
        preferred_element_type=jnp.float32,
    )
    select_out = (
        mine_local[:, :, None] == jnp.arange(stored_factors, dtype=jnp.int32)[None, None, :]
    ).astype(jnp.float32)
    delta_rows = jnp.sum(widened_rows * select_out[:, :, :, None], axis=2).astype(jnp.bfloat16)
    returned_rows = lax.all_to_all(delta_rows, "adapter", split_axis=2, concat_axis=1, tiled=True)
    my_targets = lax.dynamic_slice_in_dim(
        slot_of, part_index * present_block_list, present_block_list, 0
    )
    target_pick = (
        my_targets[:, :, None] == jnp.arange(owners * capacity, dtype=jnp.int32)[None, None, :]
    ).astype(jnp.bfloat16)
    adapter_delta_rows = jnp.einsum(
        "prs,psd->prd", target_pick, returned_rows, preferred_element_type=jnp.float32
    )
    adapter_delta_rows = adapter_delta_rows.reshape(
        present_block_list * block_of_rows, returned_rows.shape[2]
    )
    return (partial_total + adapter_delta_rows).astype(jnp.bfloat16)


def solution(mesh):
    placed = (
        P(("groups", "adapter"), ("tensor", "seq")),
        P(("tensor", "seq"), "adapter"),
        P("adapter", ("tensor", "seq"), None),
        P("adapter", None, None),
        P("groups"),
        P("groups"),
    )
    small = mesh.shape["adapter"] == 4 and mesh.shape["tensor"] == 2 and mesh.shape["seq"] == 2
    return jax.shard_map(
        small_body if small else body,
        mesh=mesh,
        in_specs=placed,
        out_specs=P(("groups", "tensor", "seq"), "adapter"),
        check_vma=False,
    )
```

```python
import functools

import jax
import jax.numpy as jnp
from jax import lax
from jax.experimental import pallas as pl
from jax.experimental.pallas import tpu as pltpu
from jax.sharding import PartitionSpec as P

F32 = jnp.float32
BF16 = jnp.bfloat16
MIB = 1024 * 1024
VMEM = pl.BlockSpec(memory_space=pltpu.VMEM)
SMEM = pl.BlockSpec(memory_space=pltpu.SMEM)
HBM = pl.BlockSpec(memory_space=pltpu.HBM)
COLUMNS = 512
FETCH_MIB = 27
SHARE = 26
MIDDLE = 12
FETCH_A = 0.01
FETCH_B = 1.0
CUT = 7
ADD_FLOPS = 8e9


def params(limit):
    return pltpu.CompilerParams(vmem_limit_bytes=limit * MIB)


def cost(flops, moved):
    return pl.CostEstimate(flops=int(flops), bytes_accessed=int(moved), transcendentals=0)


def fetch_kernel(*refs, pieces):
    count = len(pieces)
    sources, targets, sems = refs[:count], refs[count : 2 * count], refs[2 * count]
    copies = []
    for source, target, (axis, start, length, cuts) in zip(sources, targets, pieces):
        step = length // cuts
        for cut in range(cuts):
            if axis == 0:
                from_ref = source.at[pl.ds(start + cut * step, step)]
                to_ref = target.at[pl.ds(cut * step, step)]
            else:
                from_ref = source.at[:, pl.ds(start + cut * step, step)]
                to_ref = target.at[:, pl.ds(cut * step, step)]
            copies.append(pltpu.make_async_copy(from_ref, to_ref, sems.at[len(copies)]))
    for copy in copies:
        copy.start()
    for copy in copies:
        copy.wait()


def fetch(arrays, pieces, name, weight=1.0):
    shapes = []
    for array, (axis, _, length, _) in zip(arrays, pieces):
        shape = list(array.shape)
        shape[axis] = length
        shapes.append(pltpu.VMEM(tuple(shape), array.dtype))
    moved = sum(2 * s.shape[0] * s.shape[1] for s in shapes)
    total = sum(piece[3] for piece in pieces)
    return pl.pallas_call(
        functools.partial(fetch_kernel, pieces=pieces),
        in_specs=[HBM] * len(arrays),
        out_specs=[VMEM] * len(arrays),
        out_shape=shapes,
        scratch_shapes=[pltpu.SemaphoreType.DMA((total,))],
        compiler_params=params(FETCH_MIB),
        cost_estimate=cost(0, weight * moved),
        name=name,
    )(*arrays)


def dot_nt(a, b):
    return lax.dot_general(a, b, (((1,), (1,)), ((), ())), preferred_element_type=F32)


def ordered(blocks, skip):
    own = lax.axis_index("adapter")
    near = (lax.axis_index("seq") ^ (own & 1)) == 1
    far = (lax.axis_index("tensor") ^ (own >> 1)) == 1
    depth = blocks[2].shape[1]
    b0, b1, b2, b3 = [
        block[...] if block.shape[1] == depth else block[:, skip : skip + depth]
        for block in blocks
    ]
    k0, k2 = jnp.where(near, b1, b0), jnp.where(near, b3, b2)
    s0, s2 = jnp.where(near, b0, b1), jnp.where(near, b2, b3)
    return jnp.concatenate(
        [
            jnp.where(far, k2, k0),
            jnp.where(far, k0, k2),
            jnp.where(far, s2, s0),
            jnp.where(far, s0, s2),
        ],
        axis=0,
    )


def first_kernel(
    b0, b1, b2, b3, w_far, w_ref, a_ref, base_ref, low_ref, streamed, sems, *, cuts, stop
):
    cut = streamed.shape[0]
    step = cut // cuts
    copies = []
    for index in range(cuts):
        rows = pl.ds(index * step, step)
        copies.append(pltpu.make_async_copy(w_far.at[rows], streamed.at[rows], sems.at[index]))
        copies[-1].start()
    h = ordered((b0, b1, b2, b3), 0)
    depth = h.shape[1]
    low_ref[...] = dot_nt(h, a_ref[:, :depth])
    for start in range(0, w_ref.shape[1], COLUMNS):
        columns = slice(start, start + COLUMNS)
        base_ref[:, columns] = jnp.dot(
            h[:, cut:stop], w_ref[: stop - cut, columns], preferred_element_type=F32
        )
    for copy in copies:
        copy.wait()
    for start in range(0, w_ref.shape[1], COLUMNS):
        columns = slice(start, start + COLUMNS)
        base_ref[:, columns] += jnp.dot(
            h[:, :cut], streamed[:, columns], preferred_element_type=F32
        )


def first_half(blocks, w_far, w, a, cut, stop):
    rows, extent = blocks[2].shape
    width, low = w.shape[1], a.shape[0]
    cuts = 4
    return pl.pallas_call(
        functools.partial(first_kernel, cuts=cuts, stop=stop),
        in_specs=[VMEM] * 4 + [HBM] + [VMEM] * 2,
        out_specs=[VMEM] * 2,
        out_shape=[
            jax.ShapeDtypeStruct((4 * rows, width), F32),
            jax.ShapeDtypeStruct((4 * rows, low), F32),
        ],
        scratch_shapes=[pltpu.VMEM((cut, width), BF16), pltpu.SemaphoreType.DMA((cuts,))],
        compiler_params=params(20),
        cost_estimate=cost(8 * rows * extent * (width + low), 4 * MIB),
        name="first_half",
    )(*blocks, w_far, w, a)


def low_kernel(b0, b1, b2, b3, a_ref, low_in, keep_ref, send_ref):
    skip = a_ref.shape[1] - b2.shape[1]
    h = ordered((b0, b1, b2, b3), skip)
    total = low_in[...] + dot_nt(h, a_ref[:, skip:])
    rows = keep_ref.shape[0]
    keep_ref[...] = total[:rows]
    send_ref[...] = total[rows:]


def second_low(blocks, a, low_in):
    rows, extent = blocks[2].shape
    low = a.shape[0]
    return pl.pallas_call(
        low_kernel,
        in_specs=[VMEM] * 6,
        out_specs=[VMEM] * 2,
        out_shape=[jax.ShapeDtypeStruct((2 * rows, low), F32)] * 2,
        compiler_params=params(8),
        cost_estimate=cost(8 * rows * extent * low, MIB),
        name="second_low",
    )(*blocks, a, low_in)


def middle_kernel(b0, b1, b2, b3, w_ref, base_in, base_ref, *, depth):
    h = ordered((b0, b1, b2, b3), 0)
    taken, held = h.shape[1] - depth, w_ref.shape[0] - depth
    for start in range(0, w_ref.shape[1], COLUMNS):
        columns = slice(start, start + COLUMNS)
        part = jnp.dot(h[:, taken:], w_ref[held:, columns], preferred_element_type=F32)
        base_ref[:, columns] = base_in[:, columns] + part


def middle_base(blocks, w, base_in, depth):
    rows = blocks[2].shape[0]
    return pl.pallas_call(
        functools.partial(middle_kernel, depth=depth),
        in_specs=[VMEM] * 6,
        out_specs=VMEM,
        out_shape=jax.ShapeDtypeStruct(base_in.shape, F32),
        compiler_params=params(8),
        cost_estimate=cost(8 * rows * depth * w.shape[1], 4 * MIB),
        name="middle_base",
    )(*blocks, w, base_in)


def base_kernel(b0, b1, b2, b3, w_ref, base_in, keep_ref, send_ref):
    h = ordered((b0, b1, b2, b3), b1.shape[1] - b2.shape[1])
    rows = keep_ref.shape[0]
    for start in range(0, w_ref.shape[1], COLUMNS):
        columns = slice(start, start + COLUMNS)
        part = jnp.dot(h, w_ref[:, columns], preferred_element_type=F32)
        total = base_in[:, columns] + part
        keep_ref[:, columns] = total[:rows]
        send_ref[:, columns] = total[rows:].astype(BF16)


def second_base(blocks, w, base_in):
    rows, extent = blocks[2].shape
    width = w.shape[1]
    return pl.pallas_call(
        base_kernel,
        in_specs=[VMEM] * 6,
        out_specs=[VMEM] * 2,
        out_shape=[
            jax.ShapeDtypeStruct((2 * rows, width), F32),
            jax.ShapeDtypeStruct((2 * rows, width), BF16),
        ],
        compiler_params=params(12),
        cost_estimate=cost(8 * rows * extent * width, 4 * MIB),
        name="second_base",
    )(*blocks, w, base_in)


def split_kernel(keep_in, came, keep_ref, send_ref):
    rows = keep_ref.shape[0]
    total = keep_in[...] + came[...].astype(F32)
    keep_ref[...] = total[:rows]
    send_ref[...] = total[rows:].astype(send_ref.dtype)


def split_sum(keep, came, name):
    shape = (keep.shape[0] // 2, keep.shape[1])
    return pl.pallas_call(
        split_kernel,
        in_specs=[VMEM] * 2,
        out_specs=[VMEM] * 2,
        out_shape=[jax.ShapeDtypeStruct(shape, F32), jax.ShapeDtypeStruct(shape, came.dtype)],
        compiler_params=params(4),
        cost_estimate=cost(0, MIB),
        name=name,
    )(keep, came)


def plan_kernel(storage, index_ref, into_ref, back_ref, *, stored, slots):
    own = lax.axis_index("adapter")
    part = lax.axis_index("tensor") * 2 + lax.axis_index("seq")
    rows = back_ref.shape[0]
    shape = (rows, index_ref.shape[1])
    spot = lax.broadcasted_iota(jnp.int32, shape, 0) + part * rows
    chosen = lax.broadcasted_iota(jnp.int32, shape, 1) == spot
    index = jnp.sum(jnp.where(chosen, index_ref[...], 0), axis=1, keepdims=True)

    def position(index):
        found = jnp.zeros_like(index)
        for adapter in range(storage.shape[0]):
            found = jnp.where(index == adapter, storage[adapter], found)
        return found

    def owner_of(place):
        owner = jnp.zeros_like(place)
        for step in range(1, 4):
            owner += (place >= step * stored).astype(jnp.int32)
        return owner

    down = lax.broadcasted_iota(jnp.int32, (rows, rows), 0)
    across = lax.broadcasted_iota(jnp.int32, (rows, rows), 1)

    def turned(column):
        return jnp.sum(jnp.where(down == across, column, 0), axis=0, keepdims=True)

    place_column = position(index)
    owner_column = owner_of(place_column)
    owner_row = turned(owner_column)
    local_row = turned(place_column - owner_column * stored)
    same = owner_column == owner_row
    rank_row = jnp.sum((same & (down < across)).astype(jnp.int32), axis=0, keepdims=True)
    rank_column = jnp.sum((same & (across < down)).astype(jnp.int32), axis=1, keepdims=True)
    slot = lax.broadcasted_iota(jnp.int32, (slots, rows), 0)
    here = (owner_row == own) & (rank_row == slot)
    for index in range(stored):
        taken = here & (local_row == index)
        into_ref[index] = jnp.where(taken, 1.0, 0.0).astype(BF16)
    lane = lax.broadcasted_iota(jnp.int32, (rows, 4 * slots), 1)
    hops = owner_column ^ own
    back_ref[...] = jnp.where(lane == hops * slots + rank_column, 1.0, 0.0).astype(BF16)


def plan(storage, index, rows, stored, slots):
    return pl.pallas_call(
        functools.partial(plan_kernel, stored=stored, slots=slots),
        in_specs=[SMEM, VMEM],
        out_specs=[VMEM] * 2,
        out_shape=[
            jax.ShapeDtypeStruct((stored, slots, rows), BF16),
            jax.ShapeDtypeStruct((rows, 4 * slots), BF16),
        ],
        compiler_params=params(2),
        cost_estimate=cost(0, MIB),
        name="plan",
    )(storage, index[None, :])


def widen_kernel(low_a, low_b, into_ref, b_ref, *outs):
    low = (low_a[...] + low_b[...]).astype(BF16)
    stored = into_ref.shape[0]
    rank_extent = low.shape[1] // stored
    terms = []
    for index in range(stored):
        part = low[:, index * rank_extent : (index + 1) * rank_extent]
        terms.append(jnp.dot(into_ref[index], part, preferred_element_type=F32).astype(BF16))
    packed = jnp.concatenate(terms, axis=1)
    width = outs[0].shape[1]
    for step, out in enumerate(outs):
        start = pl.multiple_of((lax.axis_index("adapter") ^ step) * width, width)
        columns = b_ref[:, pl.ds(start, width)]
        out[...] = jnp.dot(packed, columns, preferred_element_type=F32).astype(BF16)


def widen(low_a, low_b, into, b, slots, owners):
    width = b.shape[1] // owners
    return pl.pallas_call(
        widen_kernel,
        in_specs=[VMEM] * 4,
        out_specs=[VMEM] * owners,
        out_shape=[jax.ShapeDtypeStruct((slots, width), BF16)] * owners,
        compiler_params=params(6),
        cost_estimate=cost(0, MIB),
        name="widen",
    )(low_a, low_b, into, b)


def add_kernel(keep, back, d0, d3, d1, d2, out_ref):
    deltas = jnp.concatenate([d[...] for d in (d0, d1, d2, d3)], axis=0)
    out_ref[...] = keep[...] + jnp.dot(back[...], deltas, preferred_element_type=F32)


def add_rows(keep, back, deltas):
    return pl.pallas_call(
        add_kernel,
        in_specs=[VMEM] * 6,
        out_specs=VMEM,
        out_shape=jax.ShapeDtypeStruct(keep.shape, F32),
        compiler_params=params(4),
        cost_estimate=cost(ADD_FLOPS, MIB),
        name="add_rows",
    )(keep, back, deltas[0], deltas[3], deltas[1], deltas[2])


def last_kernel(keep, came, out_ref):
    out_ref[...] = (keep[...] + came[...].astype(F32)).astype(out_ref.dtype)


def last(keep, came):
    return pl.pallas_call(
        last_kernel,
        in_specs=[VMEM] * 2,
        out_specs=VMEM,
        out_shape=jax.ShapeDtypeStruct(keep.shape, BF16),
        compiler_params=params(4),
        cost_estimate=cost(0, MIB),
        name="last",
    )(keep, came)


def small_body(
    hidden, down_matrix, adapter_first_factors, adapter_second_factors, adapter_index_rows, storage
):
    owners = 4
    rows, extent = hidden.shape
    stored, _, rank_extent = adapter_first_factors.shape
    slots = max(2, min(rows // 2, 2 * rows // owners))
    half = 128 * (extent * SHARE // (128 * 56))
    cut = 128 * (extent * CUT // (128 * 56))
    middle = 128 * (extent * MIDDLE // (128 * 56))
    rest = extent - half

    a = jnp.swapaxes(adapter_first_factors, 1, 2).reshape(stored * rank_extent, extent)
    b = adapter_second_factors.reshape(stored * rank_extent, -1)
    pairs = [(0, 1), (1, 0), (2, 3), (3, 2)]
    twos = [(0, 2), (2, 0), (1, 3), (3, 1)]
    both = [(0, 1), (1, 0)]
    hop = functools.partial(lax.ppermute, axis_name="adapter")

    barrier = lax.optimization_barrier
    h0 = hidden
    h1 = hop(h0, perm=pairs)
    h0a = hidden[:, :half]
    h2a = hop(h0a, perm=twos)
    (h0b,) = fetch((hidden,), ((1, half, rest, 1),), "half_b")
    h0b, down_matrix = barrier((h0b, down_matrix))
    (w_b,) = fetch((down_matrix,), ((0, half, rest, 8),), "fetch_b", FETCH_B)
    w_b, down_matrix = barrier((w_b, down_matrix))
    h2b = hop(h0b, perm=twos)
    h2a, w_b, down_matrix, adapter_index_rows = barrier((h2a, w_b, down_matrix, adapter_index_rows))
    h3a = hop(h2a, perm=pairs)
    (w_a,) = fetch(
        (down_matrix,),
        ((0, cut, half - cut, 4),),
        "fetch_a",
        FETCH_A,
    )
    into, back = plan(storage, adapter_index_rows, rows, stored, slots)
    h2b, into, back, w_a = barrier((h2b, into, back, w_a))
    h3b = hop(h2b, perm=pairs)

    blocks_a = (h0, h1, h2a, h3a)
    base_a, low_a = first_half(blocks_a, down_matrix, w_a, a, cut, half - middle)
    h3b, base_a, low_a = barrier((h3b, base_a, low_a))
    blocks_b = (h0, h1, h2b, h3b)
    low_keep, low_send = second_low(blocks_b, a, low_a)
    w_a, low_keep = barrier((w_a, low_keep))
    low_came = lax.ppermute(low_send, "seq", both)
    base_a = middle_base(blocks_a, w_a, base_a, middle)
    low_came, base_a = barrier((low_came, base_a))
    low_keep, low_send = split_sum(low_keep, low_came, "split_low")
    low_came = lax.ppermute(low_send, "tensor", both)
    w_b, low_keep = barrier((w_b, low_keep))
    base_keep, base_send = second_base(blocks_b, w_b, base_a)
    base_keep, low_came = barrier((base_keep, low_came))
    wide = widen(low_keep, low_came, into, b, slots, owners)
    base_send, wide = barrier((base_send, wide))
    base_came = lax.ppermute(base_send, "seq", both)
    deltas = {0: wide[0]}
    for step in (1, 2, 3):
        deltas[step] = hop(wide[step], perm=[(i, i ^ step) for i in range(owners)])
    deltas = [deltas[step] for step in range(owners)]
    base_keep, base_send = split_sum(base_keep, base_came, "split_base")
    base_came = lax.ppermute(base_send, "tensor", both)
    return last(add_rows(base_keep, back, deltas), base_came)


def body(
    hidden, down_matrix, adapter_first_factors, adapter_second_factors, adapter_index_rows, storage
):
    owners = lax.axis_size("adapter")
    groups = lax.axis_size(("tensor", "seq"))
    block_of_rows = hidden.shape[0]
    slice_width = hidden.shape[1]
    stored_factors = adapter_first_factors.shape[0]
    rank_extent = adapter_first_factors.shape[2]
    adapters = storage.shape[0]
    capacity = max(2, min(block_of_rows // 2, 2 * block_of_rows // owners))
    present_block_list = owners // groups
    own_index = lax.axis_index("adapter")
    part_index = lax.axis_index(("tensor", "seq"))
    id_match = adapter_index_rows[:, None] == jnp.arange(adapters, dtype=jnp.int32)[None, :]
    position = jnp.sum(jnp.where(id_match, storage[None, :], 0), axis=1)
    owner_blocks = (position // stored_factors).reshape(owners, block_of_rows)
    local_blocks = (position % stored_factors).reshape(owners, block_of_rows)
    owner_hits = (
        owner_blocks[:, :, None] == jnp.arange(owners, dtype=jnp.int32)[None, None, :]
    ).astype(jnp.int32)
    slot_rank = jnp.sum(owner_hits * (jnp.cumsum(owner_hits, axis=1) - 1), axis=2)
    slot_of = owner_blocks * capacity + slot_rank
    slot_range = jnp.arange(capacity, dtype=jnp.int32)
    owned = owner_blocks == own_index
    picker = owned[:, None, :] & (slot_rank[:, None, :] == slot_range[None, :, None])
    local_in = jnp.sum(jnp.where(picker, local_blocks[:, None, :], 0), axis=2)
    h_all = lax.all_gather(hidden, "adapter", axis=0, tiled=True)
    partial_total = lax.psum_scatter(
        jnp.dot(h_all, down_matrix, preferred_element_type=jnp.float32),
        ("tensor", "seq"),
        scatter_dimension=0,
        tiled=True,
    )
    my_slots = lax.dynamic_index_in_dim(slot_of, own_index, 0, keepdims=False)
    send_pick = my_slots[None, :] == jnp.arange(owners * capacity, dtype=jnp.int32)[:, None]
    send_rows = jnp.dot(send_pick.astype(jnp.bfloat16), hidden, preferred_element_type=jnp.float32)
    send_rows = send_rows.astype(jnp.bfloat16).reshape(owners, capacity, slice_width)
    input_rows = lax.all_to_all(send_rows, "adapter", split_axis=0, concat_axis=0, tiled=True)
    product_terms = jnp.einsum(
        "mbw,twk->mbtk", input_rows, adapter_first_factors, preferred_element_type=jnp.float32
    )
    product_terms = product_terms.reshape(
        input_rows.shape[0], input_rows.shape[1], stored_factors * rank_extent
    )
    select_low = (
        local_in[:, :, None] == jnp.arange(stored_factors, dtype=jnp.int32)[None, None, :]
    ).astype(jnp.float32)
    low_part = jnp.sum(
        product_terms.reshape(owners, capacity, stored_factors, rank_extent)
        * select_low[:, :, :, None],
        axis=2,
    )
    low_rank = lax.psum(low_part, ("tensor", "seq")).astype(jnp.bfloat16)
    owned_lowrank_part = lax.dynamic_slice_in_dim(
        low_rank, part_index * present_block_list, present_block_list, 0
    )
    mine_local = lax.dynamic_slice_in_dim(
        local_in, part_index * present_block_list, present_block_list, 0
    )
    widened_rows = jnp.einsum(
        "jwf,sfe->jwse",
        owned_lowrank_part,
        adapter_second_factors,
        preferred_element_type=jnp.float32,
    )
    select_out = (
        mine_local[:, :, None] == jnp.arange(stored_factors, dtype=jnp.int32)[None, None, :]
    ).astype(jnp.float32)
    delta_rows = jnp.sum(widened_rows * select_out[:, :, :, None], axis=2).astype(jnp.bfloat16)
    returned_rows = lax.all_to_all(delta_rows, "adapter", split_axis=2, concat_axis=1, tiled=True)
    my_targets = lax.dynamic_slice_in_dim(
        slot_of, part_index * present_block_list, present_block_list, 0
    )
    target_pick = (
        my_targets[:, :, None] == jnp.arange(owners * capacity, dtype=jnp.int32)[None, None, :]
    ).astype(jnp.bfloat16)
    adapter_delta_rows = jnp.einsum(
        "prs,psd->prd", target_pick, returned_rows, preferred_element_type=jnp.float32
    )
    adapter_delta_rows = adapter_delta_rows.reshape(
        present_block_list * block_of_rows, returned_rows.shape[2]
    )
    return (partial_total + adapter_delta_rows).astype(jnp.bfloat16)


def solution(mesh):
    placed = (
        P(("groups", "adapter"), ("tensor", "seq")),
        P(("tensor", "seq"), "adapter"),
        P("adapter", ("tensor", "seq"), None),
        P("adapter", None, None),
        P("groups"),
        P("groups"),
    )
    small = mesh.shape["adapter"] == 4 and mesh.shape["tensor"] == 2 and mesh.shape["seq"] == 2
    return jax.shard_map(
        small_body if small else body,
        mesh=mesh,
        in_specs=placed,
        out_specs=P(("groups", "tensor", "seq"), "adapter"),
        check_vma=False,
    )
```
